256 devices in a mesh: seq: 32 (over z, x), dp: 8 (over y, core).
Axes of the slice: x: 4, y: 4, z: 8, core: 2. Of those that a mesh axis runs over, the one named last changes fastest.
Arguments:
- queries: bfloat16 [8, 12288, 1536], P('dp', 'seq'), may hold values from -256 to 256
- keys: bfloat16 [8, 12288, 1536], P('dp', 'seq'), may hold values from -6 to 6
- values: bfloat16 [8, 12288, 1536], P('dp', 'seq'), may hold values from -6 to 6
- cotangent: bfloat16 [8, 12288, 3072], P('dp', 'seq'), may hold values from -0.119628906 to 0.119628906
- adapter_down_weight: bfloat16 [1536, 64], replicated, may hold values from -0.15625 to 0.15625
- adapter_up_weight: bfloat16 [64, 3072], replicated, may hold values from -0.75 to 0.75
- tile_per_slot_block: int32 [8, 32], P('dp'), may hold values from 0 to 31, as said below
- tile_window_table: int32 [8, 32, 6], P('dp'), may hold values from -1 to 31, as said below
- real_token_count: int32 [8, 32], P('dp'), may hold values from 192 to 384
Outputs:
- attention: bfloat16 [8, 12288, 1536], P('dp', 'seq')
- grad_a: float32 [1536, 64], replicated
- grad_b: float32 [64, 3072], replicated
The draws below stay inside these ranges and needn't reach their ends.
Inputs may be any that keep to these rules, and one draw needn't show every extreme that they name: `tile_per_slot_block`: tiles 2r and 2r+1 form pair r; slot blocks 2r and 2r+1 hold the two tiles of pair r, in either order. `tile_window_table`: tile t lies in frame-tile t // 8, tile row (t % 8) // 2 and column t % 2, and pair t // 2 is its row. Entry 0 of tile t's window is t, entry 1 the other tile of its pair; entries 2 to 5 are the two tiles of each of two other rows of the same frame-tile, within two rows of t's row, listed row by row, or -1 for a row that the window leaves out at an edge of the frame-tile.
All inputs are finite; a program needn't handle non-finite values.
Results may differ from the reference program's by a relative error of at most 0.013.
Values may be sent and summed in bfloat16 or wider, within the bound.
A program may use at most 128 MiB of HBM per device.

```python
import jax
import jax.numpy as jnp
from jax import lax

HEADS = 12
HEAD = 128
MODEL_WIDTH = 3072
ADAPTER_RANK = 64
TILE = 384
ROWS = 4
WIN = 6
HEAD_FEATURES = 1536
TILES = 32
FRAME_TILES = 4
TOKENS = 12288
N_DP = 8


def shared_rows(key):
    base = jax.random.normal(jax.random.fold_in(key, 11), (N_DP, TOKENS, HEADS * HEAD), jnp.float32)
    return jnp.clip(base, -6.0, 6.0)


def draw_keys(key, part):
    rows = shared_rows(key)
    return rows.astype(jnp.bfloat16)


def draw_queries(key, part):
    key = jax.random.fold_in(key, 1)
    shape = (N_DP, TOKENS, HEADS * HEAD)
    base = jnp.clip(2.0 * jax.random.normal(key, shape, jnp.float32), -12.0, 12.0)
    return jnp.clip(base, -256.0, 256.0).astype(jnp.bfloat16)


def draw_tile_per_slot_block(key, part):
    key = jax.random.fold_in(key, 3)
    flips = jax.random.randint(key, (N_DP, TILES // 2), 0, 2)
    index = jnp.arange(TILES, dtype=jnp.int32)
    turned = flips[:, index // 2]
    return (index[None, :] + (1 - 2 * (index % 2))[None, :] * turned).astype(jnp.int32)


def draw_tile_window_table(key, part):
    key = jax.random.fold_in(key, 4)
    tile = jnp.arange(TILES, dtype=jnp.int32)
    span = 2 * ROWS
    frame = tile // span
    row = tile % span // 2
    side = jax.random.randint(key, (N_DP, FRAME_TILES), 0, 2).astype(jnp.int32)
    side_of = side[:, frame]
    row_b = jnp.broadcast_to(row[None, :], (N_DP, TILES))
    first = jnp.where(row_b == 0, 1, jnp.where(row_b == ROWS - 1, ROWS - 2, row_b - 1))
    second = jnp.where(row_b == 0, jnp.where(side_of == 0, 2, -1), jnp.where(row_b == ROWS - 1, jnp.where(side_of == 1, ROWS - 3, -1), row_b + 1))
    base = (frame * span)[None, :]

    def tiles_of(which):
        left = jnp.where(which >= 0, base + 2 * which, -1)
        right = jnp.where(which >= 0, left + 1, -1)
        return [left, right]
    own = jnp.broadcast_to(tile[None, :], (N_DP, TILES))
    partner = jnp.bitwise_xor(own, 1)
    listed = [own, partner] + tiles_of(first) + tiles_of(second)
    return jnp.stack(listed, axis=2).astype(jnp.int32)


def draw_real_token_count(key, part):
    key = jax.random.fold_in(key, 5)
    counts = jax.random.randint(key, (N_DP, TILES), TILE // 2, TILE + 1)
    where_full = jax.random.randint(jax.random.fold_in(key, 7), (N_DP, 1), 0, TILES)
    index = jnp.arange(TILES, dtype=jnp.int32)[None, :]
    counts = jnp.where(index == where_full, TILE, counts)
    counts = jnp.where(index == (where_full + 1) % TILES, TILE // 2, counts)
    return counts.astype(jnp.int32)


def block_levels(stream_key, shape, pieces, smallest, high):
    def one(dim, parts):
        draws = jax.random.uniform(jax.random.fold_in(jax.random.fold_in(stream_key, 6), dim), (parts,), jnp.float32, smallest / len(pieces), high / len(pieces))
        return jnp.repeat(jnp.exp(draws), shape[dim] // parts).reshape((-1,) + (1,) * (len(shape) - dim - 1))

    level = one(*pieces[0])
    for cut in pieces[1:]:
        level = level * one(*cut)
    return level


def normal_values(own_key, extent, deviation, reach, pieces=(), kind=jnp.bfloat16):
    entries = jax.random.normal(own_key, extent, jnp.float32) * deviation
    if len(pieces) > 0:
        entries = block_levels(own_key, extent, pieces, -0.22, 0.18) * entries
    return jnp.clip(entries, min=-reach, max=reach).astype(kind)


def setup_inputs(seed: int = 0) -> dict:
    seeds = jax.random.split(jax.random.key(seed), 10)
    return {
        "queries": draw_queries(jax.random.fold_in(seeds[9], 71), 0),
        "keys": draw_keys(jax.random.fold_in(seeds[9], 71), 0),
        "values": normal_values(seeds[2], (N_DP, TOKENS, HEAD_FEATURES), 1.0, 6.0, ((0, 8), (1, 32))),
        "cotangent": normal_values(seeds[3], (N_DP, TOKENS, MODEL_WIDTH), 0.02, 0.119628906, ((0, 8), (1, 32))),
        "adapter_down_weight": normal_values(seeds[4], (HEAD_FEATURES, ADAPTER_RANK), HEAD_FEATURES ** -0.5, 0.15625),
        "adapter_up_weight": normal_values(seeds[5], (ADAPTER_RANK, MODEL_WIDTH), ADAPTER_RANK ** -0.5, 0.75),
        "tile_per_slot_block": draw_tile_per_slot_block(jax.random.fold_in(seeds[9], 71), 0),
        "tile_window_table": draw_tile_window_table(jax.random.fold_in(seeds[9], 71), 0),
        "real_token_count": draw_real_token_count(jax.random.fold_in(seeds[9], 71), 0),
    }


def attend(query, key_rows, value_rows, key_mask):
    scale = HEAD ** -0.5

    def one_head(index):
        start = index * HEAD
        qh = lax.dynamic_slice_in_dim(query, start, HEAD, 1)
        kh = lax.dynamic_slice_in_dim(key_rows, start, HEAD, 1)
        vh = lax.dynamic_slice_in_dim(value_rows, start, HEAD, 1)
        scores = lax.dot_general(qh, kh, (((1,), (1,)), ((), ())), preferred_element_type=jnp.float32) * scale
        scores = jnp.where(key_mask[None, :], scores, jnp.float32(-1e30))
        top = jnp.max(scores, axis=1, keepdims=True)
        expo = jnp.exp(scores - top)
        total = jnp.sum(expo, axis=1, keepdims=True)
        weights = expo.astype(jnp.bfloat16)
        return jnp.dot(weights, vh, preferred_element_type=jnp.float32) / total

    heads_out = lax.map(one_head, jnp.arange(HEADS, dtype=jnp.int32))
    return jnp.transpose(heads_out, (1, 0, 2)).reshape(query.shape[0], HEADS * HEAD)


def reference(queries, keys, values, cotangent, adapter_down_weight, adapter_up_weight, tile_per_slot_block, tile_window_table, real_token_count):
    slots = jnp.arange(TILE, dtype=jnp.int32)
    width = HEADS * HEAD

    def one_video(video):
        order = tile_per_slot_block[video]
        owner = jnp.zeros((TILES,), jnp.int32).at[order].set(jnp.arange(TILES, dtype=jnp.int32))
        q_tiles = queries[video].reshape(TILES, TILE, width)
        k_tiles = keys[video].reshape(TILES, TILE, width)
        v_tiles = values[video].reshape(TILES, TILE, width)
        valid = real_token_count[video]

        def one_slot(slot):
            tile = order[slot]
            window = tile_window_table[video, tile]
            present = window >= 0
            safe = jnp.where(present, window, 0).astype(jnp.int32)
            where_from = owner[safe]
            key_rows = k_tiles[where_from].reshape(WIN * TILE, width)
            value_rows = v_tiles[where_from].reshape(WIN * TILE, width)
            key_mask = (present[:, None] & (slots[None, :] < valid[safe][:, None])).reshape(-1)
            block_output = attend(q_tiles[slot], key_rows, value_rows, key_mask)
            block_output = jnp.where((slots < valid[tile])[:, None], block_output, jnp.float32(0.0))
            return block_output.astype(jnp.bfloat16)

        return lax.map(one_slot, jnp.arange(TILES, dtype=jnp.int32)).reshape(TOKENS, width)

    attention = lax.map(one_video, jnp.arange(N_DP, dtype=jnp.int32))
    flattened_rows = attention.reshape(N_DP * TOKENS, width)
    incoming_gradients = cotangent.reshape(N_DP * TOKENS, MODEL_WIDTH)
    hidden_state = jnp.dot(flattened_rows, adapter_down_weight, preferred_element_type=jnp.float32).astype(jnp.bfloat16)
    backward_pass = lax.dot_general(incoming_gradients, adapter_up_weight, (((1,), (1,)), ((), ())), preferred_element_type=jnp.float32).astype(jnp.bfloat16)
    grad_b = lax.dot_general(hidden_state, incoming_gradients, (((0,), (0,)), ((), ())), preferred_element_type=jnp.float32)
    grad_a = lax.dot_general(flattened_rows, backward_pass, (((0,), (0,)), ((), ())), preferred_element_type=jnp.float32)
    return attention, grad_a, grad_b
```

```python
import functools
import math

import jax
import jax.numpy as jnp
from jax import lax
from jax.experimental import pallas as pl
from jax.experimental.pallas import tpu as pltpu
from jax.sharding import PartitionSpec as P

HEAD = 128
TILE = 384
WIN = 6
CHUNKS = 3
X, Z, Y = 4, 8, 4
SCALE = math.log2(math.e) / math.sqrt(HEAD)
NT = (((1,), (1,)), ((), ()))
TN = (((0,), (0,)), ((), ()))
MESH = pl.DeviceIdType.MESH
BF16, F32 = jnp.bfloat16, jnp.float32
VMEM_LIMIT = 58 * 2**20


def place():
    seq, dp = lax.axis_index("seq"), lax.axis_index("dp")
    return seq // X, seq % X, dp // 2, dp % 2


def device(z, x, y, core):
    return {"seq": z * X + x, "dp": y * 2 + core}


def columns(head):
    return pl.ds(pl.multiple_of(head * HEAD, HEAD), HEAD)


def attend_kernel(
    order, window, valid, q_in, k_in, v_in, cot_in, down, up,
    att_out, gb_out, ga_out,
    k_0, k_1, k_2, v_0, v_1, v_2, qbuf, obuf, att, cot, back, hidden,
    s_k, r_k, s_v, r_v, s_q, r_q, s_c, r_c, s_o, r_o, s_b, r_b, l_own, l_cot, l_att,
):
    kbuf, vbuf = (k_0, k_1, k_2), (v_0, v_1, v_2)
    z, x, y, core = place()
    plane = z % 2
    here = plane * X + x
    others = ((x + 2) % X, x + 1 - 2 * (x % 2), X - 1 - x)
    over_z = device(z + 1 - 2 * plane, x, y, core)

    def own(j, which):
        src = (k_in, v_in, q_in)[which].at[0, :, columns(X * j + x)]
        dst = (kbuf[j].at[here], vbuf[j].at[here], qbuf.at[j, x])[which]
        return pltpu.make_async_copy(src, dst, l_own.at[j, which])

    def spread(j, which, rel):
        there = others[rel]
        src = (k_in, v_in, q_in)[which].at[0, :, columns(X * j + there)]
        dst = (kbuf[j].at[here], vbuf[j].at[here], qbuf.at[j, x])[which]
        return pltpu.make_async_remote_copy(
            src_ref=src, dst_ref=dst,
            send_sem=(s_k, s_v, s_q)[which].at[j, rel],
            recv_sem=(r_k, r_v, r_q)[which].at[j, rel],
            device_id=device(z, there, y, core), device_id_type=MESH,
        )

    def across(j, which, rel):
        slot = plane * X + (others + (x,))[rel]
        ref = (kbuf, vbuf)[which][j].at[slot]
        return pltpu.make_async_remote_copy(
            src_ref=ref, dst_ref=ref,
            send_sem=s_c.at[j, which, rel], recv_sem=r_c.at[j, which, rel],
            device_id=over_z, device_id_type=MESH,
        )

    def result(j, rel, there):
        return pltpu.make_async_remote_copy(
            src_ref=obuf.at[j, rel], dst_ref=att.at[:, columns(X * j + x)],
            send_sem=s_o.at[j, rel], recv_sem=r_o.at[j, rel],
            device_id=device(z, there, y, core), device_id_type=MESH,
        )

    def share(rel):
        return pltpu.make_async_remote_copy(
            src_ref=back.at[x], dst_ref=back.at[x],
            send_sem=s_b.at[rel], recv_sem=r_b.at[rel],
            device_id=device(z, others[rel], y, core), device_id_type=MESH,
        )

    def write_out(j):
        part = pl.ds(X * HEAD * j, X * HEAD)
        return pltpu.make_async_copy(att.at[:, part], att_out.at[0, :, part], l_att.at[j])

    def issue(j, which):
        for rel in range(3):
            spread(j, which, rel).start()

    def forward(j):
        for rel in (1, 2, 0):
            for which in range(2):
                spread(j, which, rel).wait_recv()
                across(j, which, rel).start()

    def forward_own(j):
        for which in range(2):
            own(j, which).wait()
            across(j, which, 3).start()

    for j in range(CHUNKS):
        for which in range(3):
            own(j, which).start()
    cot_copy = pltpu.make_async_copy(cot_in.at[0], cot, l_cot)
    cot_copy.start()

    barrier = pltpu.get_barrier_semaphore()
    for there in others:
        pl.semaphore_signal(barrier, inc=1, device_id=device(z, there, y, core), device_id_type=MESH)
    pl.semaphore_signal(barrier, inc=1, device_id=over_z, device_id_type=MESH)
    pl.semaphore_wait(barrier, 4)

    issue(0, 0)
    issue(0, 1)
    forward_own(0)
    issue(1, 0)
    issue(1, 1)
    forward_own(1)
    issue(0, 2)
    forward(0)
    issue(2, 0)
    issue(2, 1)
    forward_own(2)
    issue(1, 2)
    issue(2, 2)
    cot_copy.wait()
    back[x] = lax.dot_general(up[...], cot[...], NT, preferred_element_type=F32).astype(BF16)
    for rel in range(3):
        share(rel).start()
    forward(1)

    def unit(j, step):
        there = jnp.where(step == 0, others[0], jnp.where(step == 1, others[1], jnp.where(step == 2, others[2], x)))
        tile = order[0, z * X + there]
        slots, biases = [], []
        lane = lax.broadcasted_iota(jnp.int32, (1, TILE), 1)
        for entry in range(WIN):
            wanted = window[0, tile, entry]
            present = wanted >= 0
            known = jnp.maximum(wanted, 0)
            first = known // 2 * 2
            slot = jnp.where(order[0, first] == known, first, first + 1) - (z // 2) * 2 * X
            slots.append(jnp.where(present, jnp.clip(slot, 0, 2 * X - 1), here))
            count = jnp.where(present, valid[0, known], 0)
            biases.append(jnp.where(lane < count, 0.0, -1e30).astype(F32))
        mine = valid[0, tile]
        half = TILE // 2
        for start in (0, half):
            query = qbuf[j, there, pl.ds(start, half), :]
            scores = []
            for entry in range(WIN):
                s = lax.dot_general(query, kbuf[j][slots[entry]], NT, preferred_element_type=F32)
                scores.append(s + biases[entry])
            top = functools.reduce(jnp.maximum, scores)
            top = jnp.max(top, axis=1, keepdims=True)
            total = None
            for entry in range(WIN):
                weights = jnp.exp2((scores[entry] - top) * SCALE).astype(BF16)
                value = vbuf[j][slots[entry]]
                value = jnp.concatenate([value, jnp.ones_like(value)], axis=1)
                part = jnp.dot(weights, value, preferred_element_type=F32)
                total = part if total is None else total + part
            row = start + lax.broadcasted_iota(jnp.int32, (half, HEAD), 0)
            out = jnp.where(row < mine, total[:, :HEAD] / total[:, HEAD:], 0.0)
            obuf[j, step, pl.ds(start, half), :] = out.astype(BF16)
        part_a = jnp.dot(back[there], obuf[j, step], preferred_element_type=F32)
        ga_out[:, j * HEAD:(j + 1) * HEAD] += part_a

        @pl.when(step < 3)
        def _():
            result(j, step, there).start()

        @pl.when(step == 3)
        def _():
            att[:, columns(X * j + x)] = obuf[j, 3]

    def collect(j):
        for rel in range(3):
            result(j, rel, others[rel]).wait_recv()
        write_out(j).start()
        part = slice(X * HEAD * j, X * HEAD * (j + 1))
        term = lax.dot_general(down[:, part], att[:, part], NT, preferred_element_type=F32)
        if j == 0:
            hidden[...] = term
        else:
            hidden[...] += term

    ga_out[...] = jnp.zeros_like(ga_out)
    for rel in range(3):
        share(rel).wait_recv()
    for j in range(CHUNKS):
        own(j, 2).wait()
        for rel in range(3):
            spread(j, 2, rel).wait_recv()
        for rel in range(4):
            for which in range(2):
                across(j, which, rel).wait_recv()

        def step_of(step, _, j=j):
            unit(j, step)
            if j == 0:
                @pl.when(step == 0)
                def _():
                    forward(2)
            return 0

        lax.fori_loop(0, X, step_of, 0)
        if j > 0:
            collect(j - 1)
    collect(CHUNKS - 1)
    gb_out[...] = jnp.dot(hidden[...].astype(BF16), cot[...], preferred_element_type=F32)
    for j in range(CHUNKS):
        write_out(j).wait()
        for rel in range(3):
            for which in range(3):
                spread(j, which, rel).wait_send()
            result(j, rel, others[rel]).wait_send()
        for rel in range(4):
            for which in range(2):
                across(j, which, rel).wait_send()
    for rel in range(3):
        share(rel).wait_send()


def attend(order, window, valid, queries, keys, values, cotangent, down, up):
    smem = pl.BlockSpec(memory_space=pltpu.SMEM)
    vmem = pl.BlockSpec(memory_space=pltpu.VMEM)
    hbm = pl.BlockSpec(memory_space=pl.ANY)
    dma = pltpu.SemaphoreType.DMA
    rank, wide = up.shape
    piece = (TILE, HEAD)
    return pl.pallas_call(
        attend_kernel,
        out_shape=(
            jax.ShapeDtypeStruct(queries.shape, BF16),
            jax.ShapeDtypeStruct((rank, wide), F32),
            jax.ShapeDtypeStruct((rank, CHUNKS * HEAD), F32),
        ),
        in_specs=[smem, smem, smem, hbm, hbm, hbm, hbm, vmem, vmem],
        out_specs=(hbm, vmem, vmem),
        scratch_shapes=[pltpu.VMEM((2 * X,) + piece, BF16)] * (2 * CHUNKS)
        + [
            pltpu.VMEM((CHUNKS, X) + piece, BF16),
            pltpu.VMEM((CHUNKS, X) + piece, BF16),
            pltpu.VMEM((TILE, CHUNKS * X * HEAD), BF16),
            pltpu.VMEM((TILE, wide), BF16),
            pltpu.VMEM((X, rank, TILE), BF16),
            pltpu.VMEM((rank, TILE), F32),
        ]
        + [dma((CHUNKS, 3))] * 6
        + [dma((CHUNKS, 2, 4))] * 2
        + [dma((CHUNKS, 3))] * 2
        + [dma((3,))] * 2
        + [dma((CHUNKS, 3)), dma, dma((CHUNKS,))],
        compiler_params=pltpu.CompilerParams(
            collective_id=0, has_side_effects=True, vmem_limit_bytes=VMEM_LIMIT
        ),
        name="attend",
    )(order, window, valid, queries, keys, values, cotangent, down, up)


def reduce_kernel(
    gb, ga, gb_out, ga_out,
    half_b, half_a, sent_b, sent_a, parts, parts_a, sums, final,
    s_0, r_0, s_1, r_1, s_a, r_a, s_2, r_2, s_3, r_3, s_4, r_4,
):
    z, x, y, core = place()
    rows = gb.shape[0] // 2
    band = rows // Y
    wide = gb.shape[1] // X
    across = device(z, x, y, 1 - core)
    square = [(dx, dy) for dx in range(X) for dy in range(Y) if (dx, dy) != (0, 0)]

    def at(dx, dy):
        return (x + dx) % X, (y + dy) % Y

    barrier = pltpu.get_barrier_semaphore()
    pl.semaphore_signal(barrier, inc=1, device_id=across, device_id_type=MESH)
    for dx, dy in square:
        tx, ty = at(dx, dy)
        pl.semaphore_signal(barrier, inc=1, device_id=device(z, tx, ty, core), device_id_type=MESH)
    for dz in range(1, Z):
        pl.semaphore_signal(barrier, inc=1, device_id=device((z + dz) % Z, x, y, core), device_id_type=MESH)
    pl.semaphore_wait(barrier, 1 + len(square) + Z - 1)

    def copy(src, dst, send, recv, to):
        return pltpu.make_async_remote_copy(
            src_ref=src, dst_ref=dst, send_sem=send, recv_sem=recv, device_id=to, device_id_type=MESH
        )

    keep = pl.ds(pl.multiple_of(core * rows, rows), rows)
    give = pl.ds(pl.multiple_of((1 - core) * rows, rows), rows)
    swaps = [
        copy(gb.at[give], half_b, s_0.at[0], r_0.at[0], across),
        copy(ga.at[give], half_a, s_0.at[1], r_0.at[1], across),
    ]
    for c in swaps:
        c.start()
    for c in swaps:
        c.wait()
    sent_b[...] = gb[keep, :] + half_b[...]
    sent_a[...] = ga[keep, :] + half_a[...]

    def band_of(ty):
        return pl.ds(pl.multiple_of(ty * band, band), band)

    def cols_of(tx):
        return pl.ds(pl.multiple_of(tx * wide, HEAD), wide)

    scatter = []
    for i, (dx, dy) in enumerate(square):
        tx, ty = at(dx, dy)
        to = device(z, tx, ty, core)
        scatter.append(
            copy(sent_b.at[band_of(ty), cols_of(tx)], parts.at[i], s_1.at[i], r_1.at[i], to)
        )
        if dx == 0:
            scatter.append(
                copy(sent_a.at[band_of(ty)], parts_a.at[dy - 1], s_a.at[dy - 1], r_a.at[dy - 1], to)
            )
    for c in scatter:
        c.start()
    for c in scatter:
        c.wait()
    piece_b = sent_b[band_of(y), cols_of(x)]
    for i in range(len(square)):
        piece_b += parts[i]
    piece_a = sent_a[band_of(y), :]
    for i in range(Y - 1):
        piece_a += parts_a[i]
    sums[z, :, :wide] = piece_b
    sums[z, :, wide:] = piece_a

    ring = [
        copy(sums.at[z], sums.at[z], s_2.at[dz - 1], r_2.at[dz - 1], device((z + dz) % Z, x, y, core))
        for dz in range(1, Z)
    ]
    for c in ring:
        c.start()
    for c in ring:
        c.wait()
    total = sums[0]
    for i in range(1, Z):
        total += sums[i]
    mine = pl.ds(pl.multiple_of(core * rows + y * band, band), band)
    final[x, mine, :] = total

    gather = [
        copy(final.at[x, mine], final.at[x, mine], s_3.at[i], r_3.at[i], device(z, *at(dx, dy), core))
        for i, (dx, dy) in enumerate(square)
    ]
    for c in gather:
        c.start()
    for c in gather:
        c.wait()
    last = copy(final.at[:, keep], final.at[:, keep], s_4.at[0], r_4.at[0], across)
    last.start()
    last.wait()
    for i in range(X):
        gb_out[:, i * wide:(i + 1) * wide] = final[i, :, :wide]
        for j in range(CHUNKS):
            head = X * j + i
            block = final[i, :, wide + j * HEAD:wide + (j + 1) * HEAD]
            ga_out[head * HEAD:(head + 1) * HEAD, :] = block.T


def reduce(gb, ga):
    vmem = pl.BlockSpec(memory_space=pltpu.VMEM)
    dma = pltpu.SemaphoreType.DMA
    rank, wide = gb.shape
    rows, band, part, part_a = rank // 2, rank // 2 // Y, wide // X, ga.shape[1]
    near = X * Y - 1
    return pl.pallas_call(
        reduce_kernel,
        out_shape=(
            jax.ShapeDtypeStruct((rank, wide), F32),
            jax.ShapeDtypeStruct((X * part_a, rank), F32),
        ),
        in_specs=[vmem, vmem],
        out_specs=(vmem, vmem),
        scratch_shapes=[
            pltpu.VMEM((rows, wide), F32),
            pltpu.VMEM((rows, part_a), F32),
            pltpu.VMEM((rows, wide), F32),
            pltpu.VMEM((rows, part_a), F32),
            pltpu.VMEM((near, band, part), F32),
            pltpu.VMEM((Y - 1, band, part_a), F32),
            pltpu.VMEM((Z, band, part + part_a), F32),
            pltpu.VMEM((X, rank, part + part_a), F32),
        ]
        + [dma((2,))] * 2
        + [dma((near,))] * 2
        + [dma((Y - 1,))] * 2
        + [dma((Z - 1,))] * 2
        + [dma((near,))] * 2
        + [dma((1,))] * 2,
        compiler_params=pltpu.CompilerParams(
            collective_id=1, has_side_effects=True, vmem_limit_bytes=VMEM_LIMIT
        ),
        name="reduce",
    )(gb, ga)


def per_device(queries, keys, values, cotangent, down, up, order, window, valid):
    attention, part_b, part_a = attend(
        order, window, valid, queries, keys, values, cotangent, down.T, up
    )
    grad_b, grad_a = reduce(part_b, part_a)
    return attention, grad_a, grad_b


def solution(mesh):
    placed = (
        P("dp", "seq", None),
        P("dp", "seq", None),
        P("dp", "seq", None),
        P("dp", "seq", None),
        P(),
        P(),
        P("dp", None),
        P("dp", None, None),
        P("dp", None),
    )
    return jax.shard_map(
        per_device,
        mesh=mesh,
        in_specs=placed,
        out_specs=(P("dp", "seq", None), P(), P()),
        check_vma=False,
    )
```

```python
import functools
import math

import jax
import jax.numpy as jnp
from jax import lax
from jax.experimental import pallas as pl
from jax.experimental.pallas import tpu as pltpu
from jax.sharding import PartitionSpec as P

HEAD = 128
HEADS = 12
TILE = 384
WIN = 6
X, Z, Y = 4, 8, 4
GROUP = 2 * X
SCALE = math.log2(math.e) / math.sqrt(HEAD)
NT = (((1,), (1,)), ((), ()))
MESH = pl.DeviceIdType.MESH
BF16, F32 = jnp.bfloat16, jnp.float32
VMEM_LIMIT = 58 * 2**20
PART_B = 384
PART_A = 256
PART = PART_B + PART_A
SQUARE = [(dx, dy) for dx in range(X) for dy in range(Y) if (dx, dy) != (0, 0)]


def place():
    seq, dp = lax.axis_index("seq"), lax.axis_index("dp")
    return seq // X, seq % X, dp // 2, dp % 2


def device(z, x, y, core):
    return {"seq": z * X + x, "dp": y * 2 + core}


def columns(head):
    return pl.ds(pl.multiple_of(head * HEAD, HEAD), HEAD)


def remote(src, dst, send, recv, to):
    return pltpu.make_async_remote_copy(
        src_ref=src, dst_ref=dst, send_sem=send, recv_sem=recv, device_id=to, device_id_type=MESH
    )


def flip(a, b):
    return a + b - 2 * a * b


def kernel(
    order, window, valid, q_in, k_in, v_in, cot_in, down_t, up,
    att_out, sum_out,
    k_four, v_four, q_four, o_four, k_eight, v_eight, q_eight, o_eight,
    k_all, v_all, q_all, att, cot, back, hidden, grad_a,
    keep, give, got, acc, parts, sums, final,
    s_four, r_four, s_z, r_z, s_eight, r_eight, s_of, r_of, s_oe, r_oe,
    l_in, l_cot, l_att, l_sum,
    s_0, r_0, s_1, r_1, s_2, r_2, s_3, r_3, s_4, r_4,
):
    z, x, y, core = place()
    frame, plane = z // 2, z % 2
    here = plane * X + x
    staged = (k_all, v_all, q_all)
    fours = (k_four, v_four, q_four)
    eights = (k_eight, v_eight, q_eight)

    def slot_of(rel):
        return (
            4 * flip(plane, rel // 4) + 2 * flip(x // 2, rel // 2 % 2) + flip(x % 2, rel % 2)
        )

    def at_slot(slot):
        return device(2 * frame + slot // X, slot % X, y, core)

    over_core = device(z, x, y, 1 - core)

    def over_square(dx, dy):
        return device(z, (x + dx) % X, (y + dy) % Y, core)

    def over_ring(dz):
        return device((z + dz) % Z, x, y, core)

    def stage(part, which):
        width = X * HEAD
        span = pl.ds(part * width, width)
        return pltpu.make_async_copy(
            (k_in, v_in, q_in)[which].at[0, :, span], staged[which].at[:, span], l_in.at[part, which]
        )

    def four(which, rel):
        slot = slot_of(rel)
        dst = fours[which].at[here if which < 2 else x]
        return remote(
            staged[which].at[:, columns(slot % X)], dst,
            s_four.at[which, rel - 1], r_four.at[which, rel - 1], at_slot(slot),
        )

    def over_z(which, rel):
        ref = fours[which].at[slot_of(rel)]
        return remote(ref, ref, s_z.at[which, rel], r_z.at[which, rel], at_slot(slot_of(4)))

    def eight(which, rel):
        slot = slot_of(rel)
        return remote(
            staged[which].at[:, columns(X + slot)], eights[which].at[here],
            s_eight.at[which, rel - 1], r_eight.at[which, rel - 1], at_slot(slot),
        )

    def out_four(rel):
        slot = slot_of(rel)
        return remote(
            o_four.at[rel], att.at[:, columns(x)], s_of.at[rel - 1], r_of.at[rel - 1], at_slot(slot)
        )

    def out_eight(rel):
        slot = slot_of(rel)
        return remote(
            o_eight.at[rel], att.at[:, columns(X + here)], s_oe.at[rel - 1], r_oe.at[rel - 1],
            at_slot(slot),
        )

    def write_out(part):
        span = pl.ds(X * HEAD * part, X * HEAD * (part + 1))
        return pltpu.make_async_copy(att.at[:, span], att_out.at[0, :, span], l_att.at[part])

    for part in range(3):
        for which in range(3):
            stage(part, which).start()
    cot_copy = pltpu.make_async_copy(cot_in.at[0], cot, l_cot)
    cot_copy.start()

    partners = [at_slot(slot_of(rel)) for rel in range(1, GROUP)] + [over_core]
    partners += [over_square(dx, dy) for dx, dy in SQUARE if dy != 0]
    barrier = pltpu.get_barrier_semaphore()
    for to in partners:
        pl.semaphore_signal(barrier, inc=1, device_id=to, device_id_type=MESH)
    for dz in range(1, Z):
        @pl.when((z + dz) % Z != 2 * frame + 1 - plane)
        def _(dz=dz):
            pl.semaphore_signal(barrier, inc=1, device_id=over_ring(dz), device_id_type=MESH)
    pl.semaphore_wait(barrier, len(partners) + Z - 2)

    for which in range(3):
        stage(0, which).wait()
    for which in range(2):
        fours[which][here] = staged[which][:, columns(x)]
        for rel in (2, 1, 3):
            four(which, rel).start()
        over_z(which, 0).start()
    for rel in (2, 1, 3):
        four(2, rel).start()
    q_four[x] = q_all[:, columns(x)]
    for part in (1, 2):
        for which in range(3):
            stage(part, which).wait()
    for which in range(2):
        for rel in (2, 1, 3):
            eight(which, rel).start()
    for rel in (1, 3, 2):
        for which in range(2):
            four(which, rel).wait_recv()
            over_z(which, rel).start()
    for which in range(2):
        for rel in (4, 6, 5, 7):
            eight(which, rel).start()
    for rel in (2, 1, 3, 4, 6, 5, 7):
        eight(2, rel).start()
    for which in range(3):
        eights[which][here] = staged[which][:, columns(X + here)]
    cot_copy.wait()
    back[...] = lax.dot_general(up[...], cot[...], NT, preferred_element_type=F32).astype(BF16)
    grad_a[:, HEADS * HEAD:] = jnp.zeros((grad_a.shape[0], HEAD), F32)

    def unit(slot, query_of, key_of, value_of, out):
        tile = order[0, 2 * X * frame + slot]
        slots, biases = [], []
        lane = lax.broadcasted_iota(jnp.int32, (1, TILE), 1)
        for entry in range(WIN):
            wanted = window[entry, 0, tile]
            present = wanted >= 0
            known = jnp.maximum(wanted, 0)
            first = known // 2 * 2
            there = jnp.where(order[0, first] == known, first, first + 1) - frame * GROUP
            slots.append(jnp.where(present, jnp.clip(there, 0, GROUP - 1), here))
            count = jnp.where(present, valid[0, known], 0)
            biases.append(jnp.where(lane < count, 0.0, -1e30).astype(F32))
        mine = valid[0, tile]
        half = TILE // 2
        for start in (0, half):
            query = query_of[pl.ds(start, half), :]
            scores = []
            for entry in range(WIN):
                s = lax.dot_general(query, key_of[slots[entry]], NT, preferred_element_type=F32)
                scores.append(s + biases[entry])
            top = jnp.max(functools.reduce(jnp.maximum, scores), axis=1, keepdims=True)
            total = None
            for entry in range(WIN):
                weights = jnp.exp2((scores[entry] - top) * SCALE).astype(BF16)
                value = value_of[slots[entry]]
                value = jnp.concatenate([value, jnp.ones_like(value)], axis=1)
                term = jnp.dot(weights, value, preferred_element_type=F32)
                total = term if total is None else total + term
            row = start + lax.broadcasted_iota(jnp.int32, (half, HEAD), 0)
            result = jnp.where(row < mine, total[:, :HEAD] / total[:, HEAD:], 0.0)
            out[pl.ds(start, half), :] = result.astype(BF16)

    def collect(first, last):
        span = slice(first * HEAD, last * HEAD)
        term = lax.dot_general(down_t[:, span], att[:, span], NT, preferred_element_type=F32)
        hidden[...] = term if first == 0 else hidden[...] + term
        grad_a[:, span] = jnp.dot(back[...], att[:, span], preferred_element_type=F32)

    for rel in range(1, X):
        four(2, rel).wait_recv()
    for rel in range(X):
        for which in range(2):
            over_z(which, rel).wait_recv()

    def four_step(step, _):
        rel = (step + 1) % X
        slot = slot_of(rel)
        unit(slot, q_four.at[slot % X], k_four, v_four, o_four.at[rel])

        @pl.when(rel != 0)
        def _():
            out_four(rel).start()

        return 0

    lax.fori_loop(0, X, four_step, 0)
    att[:, columns(x)] = o_four[0]

    for which in range(2):
        for rel in range(1, GROUP):
            eight(which, rel).wait_recv()

    def eight_step(step, _):
        rel = (step + 1) % GROUP
        slot = slot_of(rel)

        @pl.when(rel != 0)
        def _():
            eight(2, rel).wait_recv()

        unit(slot, q_eight.at[slot], k_eight, v_eight, o_eight.at[rel])

        @pl.when(rel != 0)
        def _():
            out_eight(rel).start()

        @pl.when(step == 3)
        def _():
            for other in range(1, X):
                out_four(other).wait_recv()
            write_out(0).start()
            collect(0, X)

        return 0

    lax.fori_loop(0, GROUP, eight_step, 0)
    att[:, columns(X + here)] = o_eight[0]
    for rel in range(1, GROUP):
        out_eight(rel).wait_recv()
    write_out(1).start()
    collect(X, HEADS)

    mix = hidden[...].astype(BF16)

    def fill(ref, owner):
        for i in range(X):
            from_b = pl.ds(pl.multiple_of((2 * i + owner) * PART_B, HEAD), PART_B)
            from_a = pl.ds(pl.multiple_of(3 * HEAD * i + PART_A * owner, HEAD), PART_A)
            ref[:, i * PART:i * PART + PART_B] = jnp.dot(
                mix, cot[:, from_b], preferred_element_type=F32
            )
            ref[:, i * PART + PART_B:(i + 1) * PART] = grad_a[:, from_a]

    fill(give, 1 - core)
    swap = remote(give, got, s_0.at[0], r_0.at[0], over_core)
    swap.start()
    fill(keep, core)
    swap.wait()
    acc[...] = (keep[...] + got[...]).astype(BF16)

    band = acc.shape[0] // Y

    def rows_of(there):
        return pl.ds(pl.multiple_of(there * band, band), band)

    def piece_of(there):
        return pl.ds(pl.multiple_of(there * PART, HEAD), PART)

    scatter = [
        remote(
            acc.at[rows_of((y + dy) % Y), piece_of((x + dx) % X)], parts.at[i],
            s_1.at[i], r_1.at[i], over_square(dx, dy),
        )
        for i, (dx, dy) in enumerate(SQUARE)
    ]
    for c in scatter:
        c.start()
    for c in scatter:
        c.wait()
    piece = acc[rows_of(y), piece_of(x)].astype(F32)
    for i in range(len(SQUARE)):
        piece += parts[i].astype(F32)
    sums[z] = piece.astype(BF16)

    ring = [
        remote(sums.at[z], sums.at[z], s_2.at[dz - 1], r_2.at[dz - 1], over_ring(dz))
        for dz in range(1, Z)
    ]
    for c in ring:
        c.start()
    for c in ring:
        c.wait()
    total = sums[0].astype(F32)
    for i in range(1, Z):
        total += sums[i].astype(F32)
    final[core, x, rows_of(y), :] = total.astype(BF16)

    gather = [
        remote(
            final.at[core, x, rows_of(y)], final.at[core, x, rows_of(y)],
            s_3.at[i], r_3.at[i], over_square(dx, dy),
        )
        for i, (dx, dy) in enumerate(SQUARE)
    ]
    for c in gather:
        c.start()
    for c in gather:
        c.wait()
    last = remote(final.at[core], final.at[core], s_4.at[0], r_4.at[0], over_core)
    last.start()
    last.wait()
    save = pltpu.make_async_copy(final, sum_out, l_sum)
    save.start()

    for part in range(2):
        write_out(part).wait()
    for which in range(3):
        for rel in range(1, X):
            four(which, rel).wait_send()
        for rel in range(1, GROUP):
            eight(which, rel).wait_send()
    for which in range(2):
        for rel in range(X):
            over_z(which, rel).wait_send()
    for rel in range(1, X):
        out_four(rel).wait_send()
    for rel in range(1, GROUP):
        out_eight(rel).wait_send()
    save.wait()


def attend_and_sum(order, window, valid, queries, keys, values, cotangent, down, up):
    smem = pl.BlockSpec(memory_space=pltpu.SMEM)
    vmem = pl.BlockSpec(memory_space=pltpu.VMEM)
    hbm = pl.BlockSpec(memory_space=pl.ANY)
    dma = pltpu.SemaphoreType.DMA
    rank, wide = up.shape
    width = HEADS * HEAD
    near = len(SQUARE)

    def tiles(count):
        return pltpu.VMEM((count, TILE, HEAD), BF16)

    return pl.pallas_call(
        kernel,
        out_shape=(
            jax.ShapeDtypeStruct(queries.shape, BF16),
            jax.ShapeDtypeStruct((2, X, rank, PART), BF16),
        ),
        in_specs=[smem, smem, smem, hbm, hbm, hbm, hbm, vmem, vmem],
        out_specs=(hbm, hbm),
        scratch_shapes=[tiles(GROUP), tiles(GROUP), tiles(X), tiles(X)]
        + [tiles(GROUP)] * 4
        + [pltpu.VMEM((TILE, width), BF16)] * 4
        + [
            pltpu.VMEM((TILE, wide), BF16),
            pltpu.VMEM((rank, TILE), BF16),
            pltpu.VMEM((rank, TILE), F32),
            pltpu.VMEM((rank, width + HEAD), F32),
        ]
        + [pltpu.VMEM((rank, X * PART), F32)] * 3
        + [
            pltpu.VMEM((rank, X * PART), BF16),
            pltpu.VMEM((near, rank // Y, PART), BF16),
            pltpu.VMEM((Z, rank // Y, PART), BF16),
            pltpu.VMEM((2, X, rank, PART), BF16),
        ]
        + [dma((3, X - 1))] * 2
        + [dma((2, X))] * 2
        + [dma((3, GROUP - 1))] * 2
        + [dma((X - 1,))] * 2
        + [dma((GROUP - 1,))] * 2
        + [dma((3, 3)), dma, dma((2,)), dma]
        + [dma((1,))] * 2
        + [dma((near,))] * 2
        + [dma((Z - 1,))] * 2
        + [dma((near,))] * 2
        + [dma((1,))] * 2,
        compiler_params=pltpu.CompilerParams(
            collective_id=0, has_side_effects=True, vmem_limit_bytes=VMEM_LIMIT
        ),
        name="attend",
    )(order, window, valid, queries, keys, values, cotangent, down, up)


def finish_kernel(att_in, sum_in, att_out, gb_out, ga_out, held, sems):
    take = pltpu.make_async_copy(att_in, held, sems.at[0])
    put = pltpu.make_async_copy(held, att_out, sems.at[1])
    take.start()
    for i in range(X):
        for core in range(2):
            first = (2 * i + core) * PART_B
            gb_out[:, first:first + PART_B] = sum_in[core, i, :, :PART_B].astype(F32)
        for j in range(3):
            core, start = j // 2, PART_B + j % 2 * HEAD
            block = sum_in[core, i, :, start:start + HEAD].astype(F32)
            ga_out[:, (3 * i + j) * HEAD:(3 * i + j + 1) * HEAD] = block
        if i == 0:
            take.wait()
            put.start()
    put.wait()


def finish(attention, summed, wide):
    vmem = pl.BlockSpec(memory_space=pltpu.VMEM)
    hbm = pl.BlockSpec(memory_space=pl.ANY)
    rank = summed.shape[2]
    return pl.pallas_call(
        finish_kernel,
        out_shape=(
            jax.ShapeDtypeStruct(attention.shape, BF16),
            jax.ShapeDtypeStruct((rank, wide), F32),
            jax.ShapeDtypeStruct((rank, HEADS * HEAD), F32),
        ),
        in_specs=[hbm, vmem],
        out_specs=(hbm, vmem, vmem),
        scratch_shapes=[pltpu.VMEM(attention.shape, BF16), pltpu.SemaphoreType.DMA((2,))],
        compiler_params=pltpu.CompilerParams(vmem_limit_bytes=VMEM_LIMIT),
        name="finish",
    )(attention, summed)


def per_device(queries, keys, values, cotangent, down, up, order, window, valid):
    attention, summed = attend_and_sum(
        order, window.transpose(2, 0, 1), valid, queries, keys, values, cotangent, down.T, up
    )
    attention, grad_b, grad_a = finish(attention, summed, up.shape[1])
    return attention, grad_a.T, grad_b


def solution(mesh):
    placed = (
        P("dp", "seq", None),
        P("dp", "seq", None),
        P("dp", "seq", None),
        P("dp", "seq", None),
        P(),
        P(),
        P("dp", None),
        P("dp", None, None),
        P("dp", None),
    )
    return jax.shard_map(
        per_device,
        mesh=mesh,
        in_specs=placed,
        out_specs=(P("dp", "seq", None), P(), P()),
        check_vma=False,
    )
```

```python
import functools
import math

import jax
import jax.numpy as jnp
from jax import lax
from jax.experimental import pallas as pl
from jax.experimental.pallas import tpu as pltpu
from jax.sharding import PartitionSpec as P

HEAD = 128
HEADS = 12
TILE = 384
WIN = 6
X, Z, Y = 4, 8, 4
GROUP = 2 * X
SCALE = math.log2(math.e) / math.sqrt(HEAD)
NT = (((1,), (1,)), ((), ()))
MESH = pl.DeviceIdType.MESH
BF16, F32 = jnp.bfloat16, jnp.float32
VMEM_LIMIT = 58 * 2**20
PART_B = 384
PART_A = 256
PART = PART_B + PART_A
FAR_FIRST = (2, 1, 3, 0)
SQUARE = [(dx, dy) for dx in FAR_FIRST for dy in (2, 1, 3, 0) if (dx, dy) != (0, 0)]


def place():
    seq, dp = lax.axis_index("seq"), lax.axis_index("dp")
    return seq // X, seq % X, dp // 2, dp % 2


def device(z, x, y, core):
    return {"seq": z * X + x, "dp": y * 2 + core}


def columns(head):
    return pl.ds(pl.multiple_of(head * HEAD, HEAD), HEAD)


def remote(src, dst, send, recv, to):
    return pltpu.make_async_remote_copy(
        src_ref=src, dst_ref=dst, send_sem=send, recv_sem=recv, device_id=to, device_id_type=MESH
    )


def flip(a, b):
    return a + b - 2 * a * b


def kernel(
    order_in, window_in, valid_in, q_in, k_in, v_in, cot_in, down_in, up_in,
    att_out, sum_out,
    order, window, valid, down_t, up,
    k_four, v_four, q_four, o_four, k_eight, v_eight, q_eight, o_eight,
    k_all, v_all, q_all, att, cot, back, hidden, grad_a,
    keep, give, got, acc, parts, sums, final,
    s_four, r_four, s_z, r_z, s_eight, r_eight, s_of, r_of, s_oe, r_oe,
    l_in, l_small, l_att, l_sum,
    s_0, r_0, s_1, r_1, s_2, r_2, s_3, r_3, s_4, r_4,
):
    z, x, y, core = place()
    frame, plane = z // 2, z % 2
    here = plane * X + x
    staged = (k_all, v_all, q_all)
    fours = (k_four, v_four, q_four)
    eights = (k_eight, v_eight, q_eight)

    def slot_of(rel):
        return (
            4 * flip(plane, rel // 4) + 2 * flip(x // 2, rel // 2 % 2) + flip(x % 2, rel % 2)
        )

    def at_slot(slot):
        return device(2 * frame + slot // X, slot % X, y, core)

    over_core = device(z, x, y, 1 - core)

    def over_ring(dz):
        return device((z + dz) % Z, x, y, core)

    def stage(part, which):
        width = X * HEAD
        span = pl.ds(part * width, width)
        return pltpu.make_async_copy(
            (k_in, v_in, q_in)[which].at[0, :, span], staged[which].at[:, span], l_in.at[part, which]
        )

    def four(which, rel):
        slot = slot_of(rel)
        dst = fours[which].at[here if which < 2 else x]
        return remote(
            staged[which].at[:, columns(slot % X)], dst,
            s_four.at[which, rel - 1], r_four.at[which, rel - 1], at_slot(slot),
        )

    def over_z(which, rel):
        ref = fours[which].at[slot_of(rel)]
        return remote(ref, ref, s_z.at[which, rel], r_z.at[which, rel], at_slot(slot_of(4)))

    def eight(which, rel):
        slot = slot_of(rel)
        return remote(
            staged[which].at[:, columns(X + slot)], eights[which].at[here],
            s_eight.at[which, rel - 1], r_eight.at[which, rel - 1], at_slot(slot),
        )

    def out_four(rel):
        slot = slot_of(rel)
        return remote(
            o_four.at[rel], att.at[:, columns(x)], s_of.at[rel - 1], r_of.at[rel - 1], at_slot(slot)
        )

    def out_eight(rel):
        slot = slot_of(rel)
        return remote(
            o_eight.at[rel], att.at[:, columns(X + here)], s_oe.at[rel - 1], r_oe.at[rel - 1],
            at_slot(slot),
        )

    def write_out(part):
        span = pl.ds(X * HEAD * part, X * HEAD * (part + 1))
        return pltpu.make_async_copy(att.at[:, span], att_out.at[0, :, span], l_att.at[part])

    partners = [at_slot(slot_of(rel)) for rel in range(1, GROUP)] + [over_core]
    partners += [device(z, (x + dx) % X, (y + dy) % Y, core) for dx, dy in SQUARE if dy != 0]
    barrier = pltpu.get_barrier_semaphore()
    for to in partners:
        pl.semaphore_signal(barrier, inc=1, device_id=to, device_id_type=MESH)
    for dz in range(1, Z):
        @pl.when((z + dz) % Z != 2 * frame + 1 - plane)
        def _(dz=dz):
            pl.semaphore_signal(barrier, inc=1, device_id=over_ring(dz), device_id_type=MESH)
    small = [
        pltpu.make_async_copy(src, dst, l_small.at[i])
        for i, (src, dst) in enumerate(
            (
                (up_in, up), (down_in, down_t), (order_in, order), (window_in, window),
                (valid_in, valid), (cot_in.at[0], cot),
            )
        )
    ]
    for part in range(3):
        for which in range(3):
            stage(part, which).start()
    for move in small:
        move.start()
    pl.semaphore_wait(barrier, len(partners) + Z - 2)

    for which in range(3):
        stage(0, which).wait()
    for which in range(2):
        fours[which][here] = staged[which][:, columns(x)]
        for rel in (2, 1, 3):
            four(which, rel).start()
            if rel == 2:
                over_z(which, 0).start()
    for part in (1, 2):
        for which in range(3):
            stage(part, which).wait()
    for which in range(3):
        eight(which, 4).start()
    q_four[x] = q_all[:, columns(x)]
    along = [four(2, rel) for rel in (2, 1, 3)]
    along += [eight(which, rel) for which in range(2) for rel in (2, 1, 3)]
    for rel in (1, 3, 2):
        for which in range(2):
            four(which, rel).wait_recv()
            over_z(which, rel).start()
            for c in along[:2 - which]:
                c.start()
            along = along[2 - which:]
    for other, rel in ((2, 6), (1, 5), (3, 7)):
        for which in range(2):
            eight(which, rel).start()
        eight(2, other).start()
    for rel in (6, 5, 7):
        eight(2, rel).start()
    for which in range(3):
        eights[which][here] = staged[which][:, columns(X + here)]
    for move in small:
        move.wait()
    back[...] = lax.dot_general(up[...], cot[...], NT, preferred_element_type=F32).astype(BF16)
    grad_a[:, HEADS * HEAD:] = jnp.zeros((grad_a.shape[0], HEAD), F32)

    def unit(slot, query_of, key_of, value_of, out):
        tile = order[0, 2 * X * frame + slot]
        slots, biases = [], []
        lane = lax.broadcasted_iota(jnp.int32, (1, TILE), 1)
        for entry in range(WIN):
            wanted = window[entry, 0, tile]
            present = wanted >= 0
            known = jnp.maximum(wanted, 0)
            first = known // 2 * 2
            there = jnp.where(order[0, first] == known, first, first + 1) - frame * GROUP
            slots.append(jnp.where(present, jnp.clip(there, 0, GROUP - 1), here))
            count = jnp.where(present, valid[0, known], 0)
            biases.append(jnp.where(lane < count, 0.0, -1e30).astype(F32))
        mine = valid[0, tile]
        half = TILE // 2
        for start in (0, half):
            query = query_of[pl.ds(start, half), :]
            scores = []
            for entry in range(WIN):
                s = lax.dot_general(query, key_of[slots[entry]], NT, preferred_element_type=F32)
                scores.append(s + biases[entry])
            top = jnp.max(functools.reduce(jnp.maximum, scores), axis=1, keepdims=True)
            total = None
            for entry in range(WIN):
                weights = jnp.exp2((scores[entry] - top) * SCALE).astype(BF16)
                value = value_of[slots[entry]]
                value = jnp.concatenate([value, jnp.ones_like(value)], axis=1)
                term = jnp.dot(weights, value, preferred_element_type=F32)
                total = term if total is None else total + term
            row = start + lax.broadcasted_iota(jnp.int32, (half, HEAD), 0)
            result = jnp.where(row < mine, total[:, :HEAD] / total[:, HEAD:], 0.0)
            out[pl.ds(start, half), :] = result.astype(BF16)

    def collect(first, last):
        span = slice(first * HEAD, last * HEAD)
        term = lax.dot_general(down_t[:, span], att[:, span], NT, preferred_element_type=F32)
        hidden[...] = term if first == 0 else hidden[...] + term
        grad_a[:, span] = jnp.dot(back[...], att[:, span], preferred_element_type=F32)

    for rel in range(1, X):
        four(2, rel).wait_recv()
    for rel in range(X):
        for which in range(2):
            over_z(which, rel).wait_recv()

    def four_step(step, _):
        rel = (step + 1) % X
        slot = slot_of(rel)
        unit(slot, q_four.at[slot % X], k_four, v_four, o_four.at[rel])

        @pl.when(rel != 0)
        def _():
            out_four(rel).start()

        return 0

    lax.fori_loop(0, X, four_step, 0)
    att[:, columns(x)] = o_four[0]

    for which in range(2):
        for rel in range(1, GROUP):
            eight(which, rel).wait_recv()

    def eight_step(step, _):
        rel = (step + 1) % GROUP
        slot = slot_of(rel)

        @pl.when(rel != 0)
        def _():
            eight(2, rel).wait_recv()

        unit(slot, q_eight.at[slot], k_eight, v_eight, o_eight.at[rel])

        @pl.when(rel != 0)
        def _():
            out_eight(rel).start()

        @pl.when(step == 3)
        def _():
            for other in range(1, X):
                out_four(other).wait_recv()
            write_out(0).start()
            collect(0, X)

        return 0

    lax.fori_loop(0, GROUP, eight_step, 0)
    att[:, columns(X + here)] = o_eight[0]
    for rel in range(1, GROUP):
        out_eight(rel).wait_recv()
    write_out(1).start()
    collect(X, HEADS)

    mix = hidden[...].astype(BF16)

    band = acc.shape[1] // Y

    def rows_of(there):
        return pl.ds(pl.multiple_of(there * band, band), band)

    def over_square(dx, dy):
        return device(z, (x + dx) % X, (y + dy) % Y, core)

    def fill(ref, dx, owner):
        i = (x + dx) % X
        from_b = pl.ds(pl.multiple_of((2 * i + owner) * PART_B, HEAD), PART_B)
        from_a = pl.ds(pl.multiple_of(3 * HEAD * i + PART_A * owner, HEAD), PART_A)
        ref[dx, :, :PART_B] = jnp.dot(mix, cot[:, from_b], preferred_element_type=F32)
        ref[dx, :, PART_B:] = grad_a[:, from_a]

    def swap(dx):
        return remote(give.at[dx], got.at[dx], s_0.at[dx], r_0.at[dx], over_core)

    scatter = [
        remote(
            acc.at[dx, rows_of((y + dy) % Y)], parts.at[i], s_1.at[i], r_1.at[i],
            over_square(dx, dy),
        )
        for i, (dx, dy) in enumerate(SQUARE)
    ]
    for dx in FAR_FIRST:
        fill(give, dx, 1 - core)
        swap(dx).start()
    for dx in FAR_FIRST:
        fill(keep, dx, core)
        swap(dx).wait_recv()
        acc[dx] = (keep[dx] + got[dx]).astype(BF16)
        for c, (to, _) in zip(scatter, SQUARE):
            if to == dx:
                c.start()
    piece = acc[0, rows_of(y)].astype(F32)
    for i in range(len(SQUARE)):
        scatter[i].wait_recv()
        piece += parts[i].astype(F32)
    sums[z] = piece.astype(BF16)

    ring = [
        remote(sums.at[z], sums.at[z], s_2.at[dz - 1], r_2.at[dz - 1], over_ring(dz))
        for dz in range(1, Z)
    ]
    for c in ring:
        c.start()
    for c in ring:
        c.wait()
    total = sums[0].astype(F32)
    for i in range(1, Z):
        total += sums[i].astype(F32)
    final[core, x, rows_of(y), :] = total.astype(BF16)

    gather = [
        remote(
            final.at[core, x, rows_of(y)], final.at[core, x, rows_of(y)],
            s_3.at[i], r_3.at[i], over_square(dx, dy),
        )
        for i, (dx, dy) in enumerate(SQUARE)
    ]
    for c in gather:
        c.start()
    for c in gather:
        c.wait_recv()
    last = remote(final.at[core], final.at[core], s_4.at[0], r_4.at[0], over_core)
    last.start()
    last.wait_recv()
    save = pltpu.make_async_copy(final, sum_out, l_sum)
    save.start()

    for part in range(2):
        write_out(part).wait()
    for which in range(3):
        for rel in range(1, X):
            four(which, rel).wait_send()
        for rel in range(1, GROUP):
            eight(which, rel).wait_send()
    for which in range(2):
        for rel in range(X):
            over_z(which, rel).wait_send()
    for rel in range(1, X):
        out_four(rel).wait_send()
    for rel in range(1, GROUP):
        out_eight(rel).wait_send()
    for dx in range(X):
        swap(dx).wait_send()
    for c in scatter + gather + [last]:
        c.wait_send()
    save.wait()


def attend_and_sum(order, window, valid, queries, keys, values, cotangent, down, up):
    hbm = pl.BlockSpec(memory_space=pl.ANY)
    dma = pltpu.SemaphoreType.DMA
    rank, wide = up.shape
    width = HEADS * HEAD
    near = len(SQUARE)

    def tiles(count):
        return pltpu.VMEM((count, TILE, HEAD), BF16)

    return pl.pallas_call(
        kernel,
        out_shape=(
            jax.ShapeDtypeStruct(queries.shape, BF16),
            jax.ShapeDtypeStruct((2, X, rank, PART), BF16),
        ),
        in_specs=[hbm] * 9,
        out_specs=(hbm, hbm),
        scratch_shapes=[pltpu.SMEM(t.shape, t.dtype) for t in (order, window, valid)]
        + [pltpu.VMEM(down.shape, BF16), pltpu.VMEM(up.shape, BF16)]
        + [tiles(GROUP), tiles(GROUP), tiles(X), tiles(X)]
        + [tiles(GROUP)] * 4
        + [pltpu.VMEM((TILE, width), BF16)] * 4
        + [
            pltpu.VMEM((TILE, wide), BF16),
            pltpu.VMEM((rank, TILE), BF16),
            pltpu.VMEM((rank, TILE), F32),
            pltpu.VMEM((rank, width + HEAD), F32),
        ]
        + [pltpu.VMEM((X, rank, PART), F32)] * 3
        + [
            pltpu.VMEM((X, rank, PART), BF16),
            pltpu.VMEM((near, rank // Y, PART), BF16),
            pltpu.VMEM((Z, rank // Y, PART), BF16),
            pltpu.VMEM((2, X, rank, PART), BF16),
        ]
        + [dma((3, X - 1))] * 2
        + [dma((2, X))] * 2
        + [dma((3, GROUP - 1))] * 2
        + [dma((X - 1,))] * 2
        + [dma((GROUP - 1,))] * 2
        + [dma((3, 3)), dma((6,)), dma((2,)), dma]
        + [dma((X,))] * 2
        + [dma((near,))] * 2
        + [dma((Z - 1,))] * 2
        + [dma((near,))] * 2
        + [dma((1,))] * 2,
        compiler_params=pltpu.CompilerParams(
            collective_id=0, has_side_effects=True, vmem_limit_bytes=VMEM_LIMIT
        ),
        name="attend",
    )(order, window, valid, queries, keys, values, cotangent, down, up)


def finish_kernel(att_in, sum_in, att_out, gb_out, ga_out, att, summed, gb, ga, sems):
    take_sum = pltpu.make_async_copy(sum_in, summed, sems.at[0])
    take_att = pltpu.make_async_copy(att_in, att, sems.at[1])
    put_att = pltpu.make_async_copy(att, att_out, sems.at[2])
    put_gb = pltpu.make_async_copy(gb, gb_out, sems.at[3])
    put_ga = pltpu.make_async_copy(ga, ga_out, sems.at[4])
    take_sum.start()
    take_att.start()
    take_sum.wait()
    for i in range(X):
        for core in range(2):
            first = (2 * i + core) * PART_B
            gb[:, first:first + PART_B] = summed[core, i, :, :PART_B].astype(F32)
    put_gb.start()
    for head in range(HEADS):
        i, j = head // 3, head % 3
        start = PART_B + j % 2 * HEAD
        ga[:, head * HEAD:(head + 1) * HEAD] = summed[j // 2, i, :, start:start + HEAD].astype(F32)
    put_ga.start()
    take_att.wait()
    put_att.start()
    put_gb.wait()
    put_ga.wait()
    put_att.wait()


def finish(attention, summed, wide):
    hbm = pl.BlockSpec(memory_space=pl.ANY)
    rank = summed.shape[2]
    shapes = ((attention.shape, BF16), ((rank, wide), F32), ((rank, HEADS * HEAD), F32))
    held = (shapes[0], (summed.shape, BF16), shapes[1], shapes[2])
    return pl.pallas_call(
        finish_kernel,
        out_shape=tuple(jax.ShapeDtypeStruct(*each) for each in shapes),
        in_specs=[hbm, hbm],
        out_specs=(hbm, hbm, hbm),
        scratch_shapes=[pltpu.VMEM(*each) for each in held] + [pltpu.SemaphoreType.DMA((5,))],
        compiler_params=pltpu.CompilerParams(vmem_limit_bytes=VMEM_LIMIT),
        name="finish",
    )(attention, summed)


def per_device(queries, keys, values, cotangent, down, up, order, window, valid):
    attention, summed = attend_and_sum(
        order, window.transpose(2, 0, 1), valid, queries, keys, values, cotangent, down.T, up
    )
    attention, grad_b, grad_a = finish(attention, summed, up.shape[1])
    return attention, grad_a.T, grad_b


def solution(mesh):
    placed = (
        P("dp", "seq", None),
        P("dp", "seq", None),
        P("dp", "seq", None),
        P("dp", "seq", None),
        P(),
        P(),
        P("dp", None),
        P("dp", None, None),
        P("dp", None),
    )
    return jax.shard_map(
        per_device,
        mesh=mesh,
        in_specs=placed,
        out_specs=(P("dp", "seq", None), P(), P()),
        check_vma=False,
    )
```

```python
import functools
import math

import jax
import jax.numpy as jnp
from jax import lax
from jax.experimental import pallas as pl
from jax.experimental.pallas import tpu as pltpu
from jax.sharding import PartitionSpec as P

HEAD = 128
HEADS = 12
TILE = 384
WIN = 6
X, Z, Y = 4, 8, 4
GROUP = 2 * X
SCALE = math.log2(math.e) / math.sqrt(HEAD)
NT = (((1,), (1,)), ((), ()))
MESH = pl.DeviceIdType.MESH
BF16, F32 = jnp.bfloat16, jnp.float32
VMEM_LIMIT = 58 * 2**20
PART_B = 384
PART_A = 256
PART = PART_B + PART_A
FAR_FIRST = (2, 1, 3, 0)
SQUARE = [(dx, dy) for dx in FAR_FIRST for dy in (2, 1, 3, 0) if (dx, dy) != (0, 0)]


def place():
    seq, dp = lax.axis_index("seq"), lax.axis_index("dp")
    return seq // X, seq % X, dp // 2, dp % 2


def device(z, x, y, core):
    return {"seq": z * X + x, "dp": y * 2 + core}


def columns(head):
    return pl.ds(pl.multiple_of(head * HEAD, HEAD), HEAD)


def remote(src, dst, send, recv, to):
    return pltpu.make_async_remote_copy(
        src_ref=src, dst_ref=dst, send_sem=send, recv_sem=recv, device_id=to, device_id_type=MESH
    )


def flip(a, b):
    return a + b - 2 * a * b


def kernel(
    order_in, window_in, valid_in, q_in, k_in, v_in, cot_in, down_in, up_in,
    att_out, sum_out,
    order, window, valid, down_t, up,
    k_four, v_four, q_four, o_four, k_eight, v_eight, q_eight, o_eight,
    k_all, v_all, q_all, att, cot, back, hidden,
    keep, give, got, acc, parts, sums, final,
    s_four, r_four, s_z, r_z, s_eight, r_eight, s_of, r_of, s_oe, r_oe,
    l_in, l_small, l_att, l_sum,
    s_0, r_0, s_1, r_1, s_2, r_2, s_3, r_3, s_4, r_4,
):
    z, x, y, core = place()
    frame, plane = z // 2, z % 2
    here = plane * X + x
    staged = (k_all, v_all, q_all)
    fours = (k_four, v_four, q_four)
    eights = (k_eight, v_eight, q_eight)

    def slot_of(rel):
        return (
            4 * flip(plane, rel // 4) + 2 * flip(x // 2, rel // 2 % 2) + flip(x % 2, rel % 2)
        )

    def at_slot(slot):
        return device(2 * frame + slot // X, slot % X, y, core)

    over_core = device(z, x, y, 1 - core)

    def over_ring(dz):
        return device((z + dz) % Z, x, y, core)

    def stage(part, which):
        width = X * HEAD
        span = pl.ds(part * width, width)
        return pltpu.make_async_copy(
            (k_in, v_in, q_in)[which].at[0, :, span], staged[which].at[:, span], l_in.at[part, which]
        )

    def four(which, rel):
        slot = slot_of(rel)
        dst = fours[which].at[here if which < 2 else x]
        return remote(
            staged[which].at[:, columns(slot % X)], dst,
            s_four.at[which, rel - 1], r_four.at[which, rel - 1], at_slot(slot),
        )

    def over_z(which, rel):
        ref = fours[which].at[slot_of(rel)]
        return remote(ref, ref, s_z.at[which, rel], r_z.at[which, rel], at_slot(slot_of(4)))

    def eight(which, rel):
        slot = slot_of(rel)
        return remote(
            staged[which].at[:, columns(X + slot)], eights[which].at[here],
            s_eight.at[which, rel - 1], r_eight.at[which, rel - 1], at_slot(slot),
        )

    def out_four(rel):
        slot = slot_of(rel)
        return remote(
            o_four.at[rel], att.at[:, columns(x)], s_of.at[rel - 1], r_of.at[rel - 1], at_slot(slot)
        )

    def out_eight(rel):
        slot = slot_of(rel)
        return remote(
            o_eight.at[rel], att.at[:, columns(X + here)], s_oe.at[rel - 1], r_oe.at[rel - 1],
            at_slot(slot),
        )

    def write_out(part):
        span = pl.ds(X * HEAD * part, X * HEAD * (part + 1))
        return pltpu.make_async_copy(att.at[:, span], att_out.at[0, :, span], l_att.at[part])

    partners = [at_slot(slot_of(rel)) for rel in range(1, GROUP)] + [over_core]
    partners += [device(z, (x + dx) % X, (y + dy) % Y, core) for dx, dy in SQUARE if dy != 0]
    barrier = pltpu.get_barrier_semaphore()
    for to in partners:
        pl.semaphore_signal(barrier, inc=1, device_id=to, device_id_type=MESH)
    for dz in range(1, Z):
        @pl.when((z + dz) % Z != 2 * frame + 1 - plane)
        def _(dz=dz):
            pl.semaphore_signal(barrier, inc=1, device_id=over_ring(dz), device_id_type=MESH)
    small = [
        pltpu.make_async_copy(src, dst, l_small.at[i])
        for i, (src, dst) in enumerate(
            (
                (up_in, up), (down_in, down_t), (order_in, order), (window_in, window),
                (valid_in, valid), (cot_in.at[0], cot),
            )
        )
    ]
    for part in range(3):
        for which in range(3):
            stage(part, which).start()
    for move in small:
        move.start()
    pl.semaphore_wait(barrier, len(partners) + Z - 2)

    for which in range(3):
        stage(0, which).wait()
    for which in range(2):
        fours[which][here] = staged[which][:, columns(x)]
        for rel in (2, 1, 3):
            four(which, rel).start()
            if rel == 2:
                over_z(which, 0).start()
    for part in (1, 2):
        for which in range(3):
            stage(part, which).wait()
    for which in range(3):
        eight(which, 4).start()
    q_four[x] = q_all[:, columns(x)]
    along = [four(2, rel) for rel in (2, 1, 3)]
    along += [eight(which, rel) for which in range(2) for rel in (2, 1, 3)]
    for rel in (1, 3, 2):
        for which in range(2):
            four(which, rel).wait_recv()
            over_z(which, rel).start()
            for c in along[:2 - which]:
                c.start()
            along = along[2 - which:]
    for other, rel in ((2, 6), (1, 5), (3, 7)):
        for which in range(2):
            eight(which, rel).start()
        eight(2, other).start()
    for rel in (6, 5, 7):
        eight(2, rel).start()
    for which in range(3):
        eights[which][here] = staged[which][:, columns(X + here)]
    for move in small:
        move.wait()
    back[...] = lax.dot_general(up[...], cot[...], NT, preferred_element_type=F32).astype(BF16)
    att[:, HEADS * HEAD:] = jnp.zeros((TILE, HEAD), BF16)

    half = TILE // 2
    lane = lax.broadcasted_iota(jnp.int32, (1, TILE), 1)
    row = lax.broadcasted_iota(jnp.int32, (half, HEAD), 0)

    def window_of(slot, key_of, value_of):
        tile = order[0, GROUP * frame + slot]
        keys, values, biases = [], [], []
        for entry in range(WIN):
            wanted = window[entry, 0, tile]
            present = wanted >= 0
            known = jnp.maximum(wanted, 0)
            first = known // 2 * 2
            there = jnp.where(order[0, first] == known, first, first + 1) - frame * GROUP
            there = jnp.where(present, jnp.clip(there, 0, GROUP - 1), here)
            count = jnp.where(present, valid[0, known], 0)
            keys.append(key_of[there])
            values.append(value_of[there])
            biases.append(jnp.where(lane < count, 0.0, -1e30).astype(F32))
        return keys, values, biases, valid[0, tile]

    def scores_of(query, keys, biases):
        scores = lax.dot_general(
            query, jnp.concatenate(keys, axis=0), NT, preferred_element_type=F32
        )
        return [scores[:, TILE * i:TILE * (i + 1)] + bias for i, bias in enumerate(biases)]

    def attend(scores, values, mine, start):
        top = jnp.max(functools.reduce(jnp.maximum, scores), axis=1, keepdims=True)
        weights = [jnp.exp2((each - top) * SCALE).astype(BF16) for each in scores]
        value = jnp.concatenate(values, axis=0)
        value = jnp.concatenate([value, jnp.ones_like(value)], axis=1)
        total = jnp.dot(jnp.concatenate(weights, axis=1), value, preferred_element_type=F32)
        return jnp.where(start + row < mine, total[:, :HEAD] / total[:, HEAD:], 0.0).astype(BF16)

    def units(tiles, key_of, value_of):
        jobs = []
        for slot, query_of, out, send in tiles:
            keys, values, biases, mine = window_of(slot, key_of, value_of)
            for start in (0, half):
                jobs.append((query_of, keys, values, biases, mine, start, out, send))
        ready = scores_of(jobs[0][0][pl.ds(0, half), :], jobs[0][1], jobs[0][3])
        for i, (_, _, values, _, mine, start, out, send) in enumerate(jobs):
            scores = ready
            if i + 1 < len(jobs):
                query_of, keys, _, biases, _, later = jobs[i + 1][:6]
                ready = scores_of(query_of[pl.ds(later, half), :], keys, biases)
            out[pl.ds(start, half), :] = attend(scores, values, mine, start)
        for tile in tiles:
            tile[3]()

    def collect(first, last):
        span = slice(first * HEAD, last * HEAD)
        term = lax.dot_general(down_t[:, span], att[:, span], NT, preferred_element_type=F32)
        hidden[...] = term if first == 0 else hidden[...] + term

    for rel in range(1, X):
        four(2, rel).wait_recv()
    for rel in range(X):
        for which in range(2):
            over_z(which, rel).wait_recv()

    def four_tile(rel):
        slot = slot_of(rel)
        send = out_four(rel).start if rel > 0 else lambda: None
        return slot, q_four.at[slot % X], o_four.at[rel], send

    units([four_tile(rel) for rel in (2, 1, 3, 0)], k_four, v_four)
    att[:, columns(x)] = o_four[0]

    for which in range(2):
        for rel in range(1, GROUP):
            eight(which, rel).wait_recv()

    def eight_tile(rel):
        slot = slot_of(rel)

        def send():
            @pl.when(rel != 0)
            def _():
                out_eight(rel).start()

        return slot, q_eight.at[slot], o_eight.at[rel], send

    def eight_pair(step, _):
        pair = (2 * step + 1, (2 * step + 2) % GROUP)
        for rel in pair:
            @pl.when(rel != 0)
            def _(rel=rel):
                eight(2, rel).wait_recv()

        units([eight_tile(rel) for rel in pair], k_eight, v_eight)

        @pl.when(step == 1)
        def _():
            for other in range(1, X):
                out_four(other).wait_recv()
            write_out(0).start()
            collect(0, X)

        return 0

    lax.fori_loop(0, GROUP // 2, eight_pair, 0)
    att[:, columns(X + here)] = o_eight[0]
    for rel in range(1, GROUP):
        out_eight(rel).wait_recv()
    write_out(1).start()
    collect(X, HEADS)

    mix = hidden[...].astype(BF16)

    band = acc.shape[1] // Y

    def rows_of(there):
        return pl.ds(pl.multiple_of(there * band, band), band)

    def over_square(dx, dy):
        return device(z, (x + dx) % X, (y + dy) % Y, core)

    def fill(ref, dx, owner):
        i = (x + dx) % X
        from_b = pl.ds(pl.multiple_of((2 * i + owner) * PART_B, HEAD), PART_B)
        from_a = pl.ds(pl.multiple_of(3 * HEAD * i + PART_A * owner, HEAD), PART_A)
        ref[dx, :, :PART_B] = jnp.dot(mix, cot[:, from_b], preferred_element_type=F32).astype(ref.dtype)
        ref[dx, :, PART_B:] = jnp.dot(
            back[...], att[:, from_a], preferred_element_type=F32
        ).astype(ref.dtype)

    def swap(dx):
        return remote(give.at[dx], got.at[dx], s_0.at[dx], r_0.at[dx], over_core)

    scatter = [
        remote(
            acc.at[dx, rows_of((y + dy) % Y)], parts.at[i], s_1.at[0], r_1.at[0],
            over_square(dx, dy),
        )
        for i, (dx, dy) in enumerate(SQUARE)
    ]
    for dx in FAR_FIRST:
        fill(give, dx, 1 - core)
        swap(dx).start()
    for dx in FAR_FIRST:
        fill(keep, dx, core)
        swap(dx).wait_recv()
        acc[dx] = (keep[dx] + got[dx].astype(F32)).astype(BF16)
        for c, (to, _) in zip(scatter, SQUARE):
            if to == dx:
                c.start()
    for part in range(2):
        write_out(part).wait()
    for which in range(3):
        for rel in range(1, X):
            four(which, rel).wait_send()
        for rel in range(1, GROUP):
            eight(which, rel).wait_send()
    for which in range(2):
        for rel in range(X):
            over_z(which, rel).wait_send()
    for rel in range(1, X):
        out_four(rel).wait_send()
    for rel in range(1, GROUP):
        out_eight(rel).wait_send()
    for dx in range(X):
        swap(dx).wait_send()
    all_parts = remote(parts, parts, s_1.at[0], r_1.at[0], over_core)
    all_parts.wait_recv()
    piece = acc[0, rows_of(y)].astype(F32)
    for i in range(len(SQUARE)):
        piece += parts[i].astype(F32)
    sums[z] = piece.astype(BF16)

    ring = [
        remote(sums.at[z], sums.at[z], s_2.at[0], r_2.at[0], over_ring(dz))
        for dz in range(1, Z)
    ]
    for c in ring:
        c.start()
    all_parts.wait_send()
    seven = sums.at[pl.ds(0, Z - 1)]
    all_ring = remote(seven, seven, s_2.at[0], r_2.at[0], over_core)
    all_ring.wait()
    total = sums[0].astype(F32)
    for i in range(1, Z):
        total += sums[i].astype(F32)
    final[core, x, rows_of(y), :] = total.astype(BF16)

    gather = [
        remote(
            final.at[core, x, rows_of(y)], final.at[core, x, rows_of(y)],
            s_3.at[dx], r_3.at[dx], over_square(dx, dy),
        )
        for i, (dx, dy) in enumerate(SQUARE)
    ]
    def pass_core(dx):
        ref = final.at[core, (x - dx + X) % X]
        return remote(ref, ref, s_4.at[dx], r_4.at[dx], over_core)

    def save(owner, dx):
        i = (x - dx + X) % X
        return pltpu.make_async_copy(final.at[owner, i], sum_out.at[owner, i], l_sum.at[owner, dx])

    gathered = []
    for dx in range(X):
        some = parts.at[pl.ds(0, Y if dx > 0 else Y - 1)]
        gathered.append(remote(some, some, s_3.at[dx], r_3.at[dx], over_core))
    for c in gather:
        c.start()
    for dx in (0, 1, 3, 2):
        gathered[dx].wait_recv()
        pass_core(dx).start()
        save(core, dx).start()
    for dx in (0, 1, 3, 2):
        pass_core(dx).wait_recv()
        save(1 - core, dx).start()
    for dx in range(X):
        gathered[dx].wait_send()
        pass_core(dx).wait_send()
        save(core, dx).wait()
        save(1 - core, dx).wait()


def attend_and_sum(order, window, valid, queries, keys, values, cotangent, down, up):
    hbm = pl.BlockSpec(memory_space=pl.ANY)
    dma = pltpu.SemaphoreType.DMA
    rank, wide = up.shape
    width = HEADS * HEAD
    near = len(SQUARE)

    def tiles(count):
        return pltpu.VMEM((count, TILE, HEAD), BF16)

    return pl.pallas_call(
        kernel,
        out_shape=(
            jax.ShapeDtypeStruct(queries.shape, BF16),
            jax.ShapeDtypeStruct((2, X, rank, PART), BF16),
        ),
        in_specs=[hbm] * 9,
        out_specs=(hbm, hbm),
        scratch_shapes=[pltpu.SMEM(t.shape, t.dtype) for t in (order, window, valid)]
        + [pltpu.VMEM(down.shape, BF16), pltpu.VMEM(up.shape, BF16)]
        + [tiles(GROUP), tiles(GROUP), tiles(X), tiles(X)]
        + [tiles(GROUP)] * 4
        + [pltpu.VMEM((TILE, width), BF16)] * 3
        + [pltpu.VMEM((TILE, width + HEAD), BF16)]
        + [
            pltpu.VMEM((TILE, wide), BF16),
            pltpu.VMEM((rank, TILE), BF16),
            pltpu.VMEM((rank, TILE), F32),
        ]
        + [pltpu.VMEM((X, rank, PART), F32)]
        + [pltpu.VMEM((X, rank, PART), BF16)] * 3
        + [
            pltpu.VMEM((near, rank // Y, PART), BF16),
            pltpu.VMEM((Z, rank // Y, PART), BF16),
            pltpu.VMEM((2, X, rank, PART), BF16),
        ]
        + [dma((3, X - 1))] * 2
        + [dma((2, X))] * 2
        + [dma((3, GROUP - 1))] * 2
        + [dma((X - 1,))] * 2
        + [dma((GROUP - 1,))] * 2
        + [dma((3, 3)), dma((6,)), dma((2,)), dma((2, X))]
        + [dma((X,))] * 2
        + [dma((1,))] * 4
        + [dma((X,))] * 4,
        compiler_params=pltpu.CompilerParams(
            collective_id=0, has_side_effects=True, vmem_limit_bytes=VMEM_LIMIT
        ),
        name="attend",
    )(order, window, valid, queries, keys, values, cotangent, down, up)


def finish_kernel(
    att_in, sum_in, att_out, gb_out, ga_out, att, summed, gb, ga, l_att, o_att, l_sum, o_gb, o_ga
):
    rows = TILE // X
    take_sum, take_att, put_att, put_gb, put_ga = [], [], [], [], []
    for i in range(X):
        span = pl.ds(i * rows, rows)
        wide, head = pl.ds(2 * PART_B * i, 2 * PART_B), pl.ds(3 * HEAD * i, 3 * HEAD)
        take_sum.append(pltpu.make_async_copy(sum_in.at[:, i], summed.at[:, i], l_sum.at[i]))
        take_att.append(pltpu.make_async_copy(att_in.at[0, span], att.at[0, span], l_att.at[i]))
        put_att.append(pltpu.make_async_copy(att.at[0, span], att_out.at[0, span], o_att.at[i]))
        put_gb.append(pltpu.make_async_copy(gb.at[:, wide], gb_out.at[:, wide], o_gb.at[i]))
        put_ga.append(pltpu.make_async_copy(ga.at[:, head], ga_out.at[:, head], o_ga.at[i]))
    for i in range(X):
        take_sum[i].start()
        take_att[i].start()
    for i in range(X):
        take_sum[i].wait()
        for core in range(2):
            first = (2 * i + core) * PART_B
            gb[:, first:first + PART_B] = summed[core, i, :, :PART_B].astype(F32)
        for j in range(3):
            first, start = (3 * i + j) * HEAD, PART_B + j % 2 * HEAD
            ga[:, first:first + HEAD] = summed[j // 2, i, :, start:start + HEAD].astype(F32)
        put_gb[i].start()
        put_ga[i].start()
        take_att[i].wait()
        put_att[i].start()
    for i in range(X):
        put_gb[i].wait()
        put_ga[i].wait()
        put_att[i].wait()


def finish(attention, summed, wide):
    hbm = pl.BlockSpec(memory_space=pl.ANY)
    rank = summed.shape[2]
    shapes = ((attention.shape, BF16), ((rank, wide), F32), ((rank, HEADS * HEAD), F32))
    held = (shapes[0], (summed.shape, BF16), shapes[1], shapes[2])
    return pl.pallas_call(
        finish_kernel,
        out_shape=tuple(jax.ShapeDtypeStruct(*each) for each in shapes),
        in_specs=[hbm, hbm],
        out_specs=(hbm, hbm, hbm),
        scratch_shapes=[pltpu.VMEM(*each) for each in held] + [pltpu.SemaphoreType.DMA((X,))] * 5,
        compiler_params=pltpu.CompilerParams(vmem_limit_bytes=VMEM_LIMIT),
        name="finish",
    )(attention, summed)


def per_device(queries, keys, values, cotangent, down, up, order, window, valid):
    attention, summed = attend_and_sum(
        order, window.transpose(2, 0, 1), valid, queries, keys, values, cotangent, down.T, up
    )
    attention, grad_b, grad_a = finish(attention, summed, up.shape[1])
    return attention, grad_a.T, grad_b


def solution(mesh):
    placed = (
        P("dp", "seq", None),
        P("dp", "seq", None),
        P("dp", "seq", None),
        P("dp", "seq", None),
        P(),
        P(),
        P("dp", None),
        P("dp", None, None),
        P("dp", None),
    )
    return jax.shard_map(
        per_device,
        mesh=mesh,
        in_specs=placed,
        out_specs=(P("dp", "seq", None), P(), P()),
        check_vma=False,
    )
```

```python
import functools
import math

import jax
import jax.numpy as jnp
from jax import lax
from jax.experimental import pallas as pl
from jax.experimental.pallas import tpu as pltpu
from jax.sharding import PartitionSpec as P

HEAD = 128
HEADS = 12
TILE = 384
WIN = 6
X, Z, Y = 4, 8, 4
GROUP = 2 * X
SCALE = math.log2(math.e) / math.sqrt(HEAD)
NT = (((1,), (1,)), ((), ()))
MESH = pl.DeviceIdType.MESH
BF16, F32 = jnp.bfloat16, jnp.float32
VMEM_LIMIT = 58 * 2**20
PART_B = 384
PART_A = 256
PART = PART_B + PART_A
FAR_FIRST = (2, 1, 3, 0)
SQUARE = [(dx, dy) for dx in FAR_FIRST for dy in (2, 1, 3, 0) if (dx, dy) != (0, 0)]


def place():
    seq, dp = lax.axis_index("seq"), lax.axis_index("dp")
    return seq // X, seq % X, dp // 2, dp % 2


def device(z, x, y, core):
    return {"seq": z * X + x, "dp": y * 2 + core}


def columns(head):
    return pl.ds(pl.multiple_of(head * HEAD, HEAD), HEAD)


def remote(src, dst, send, recv, to):
    return pltpu.make_async_remote_copy(
        src_ref=src, dst_ref=dst, send_sem=send, recv_sem=recv, device_id=to, device_id_type=MESH
    )


def flip(a, b):
    return a + b - 2 * a * b


def kernel(
    order_in, window_in, valid_in, q_in, k_in, v_in, cot_in, down_in, up_in,
    att_out, sum_out,
    order, window, valid, down_t, up,
    k_four, v_four, q_four, o_four, k_eight, v_eight, q_eight, o_eight,
    k_all, v_all, q_all, att, cot, back, hidden,
    keep, give, got, acc, parts, sums, final,
    s_four, r_four, s_z, r_z, s_eight, r_eight, s_of, r_of, s_oe, r_oe,
    l_in, l_small, l_att, l_sum,
    s_0, r_0, s_1, r_1, s_2, r_2, s_3, r_3, s_4, r_4,
):
    z, x, y, core = place()
    frame, plane = z // 2, z % 2
    here = plane * X + x
    staged = (k_all, v_all, q_all)
    fours = (k_four, v_four, q_four)
    eights = (k_eight, v_eight, q_eight)

    def slot_of(rel):
        return (
            4 * flip(plane, rel // 4) + 2 * flip(x // 2, rel // 2 % 2) + flip(x % 2, rel % 2)
        )

    def at_slot(slot):
        return device(2 * frame + slot // X, slot % X, y, core)

    over_core = device(z, x, y, 1 - core)

    def over_ring(dz):
        return device((z + dz) % Z, x, y, core)

    def stage(part, which):
        width = X * HEAD
        span = pl.ds(part * width, width)
        return pltpu.make_async_copy(
            (k_in, v_in, q_in)[which].at[0, :, span], staged[which].at[:, span], l_in.at[part, which]
        )

    def four(which, rel):
        slot = slot_of(rel)
        dst = fours[which].at[here if which < 2 else x]
        return remote(
            staged[which].at[:, columns(slot % X)], dst,
            s_four.at[which, rel - 1], r_four.at[which, rel - 1], at_slot(slot),
        )

    def over_z(which, rel):
        ref = fours[which].at[slot_of(rel)]
        return remote(ref, ref, s_z.at[which, rel], r_z.at[which, rel], at_slot(slot_of(4)))

    def eight(which, rel):
        slot = slot_of(rel)
        return remote(
            staged[which].at[:, columns(X + slot)], eights[which].at[here],
            s_eight.at[which, rel - 1], r_eight.at[which, rel - 1], at_slot(slot),
        )

    def out_four(rel):
        slot = slot_of(rel)
        return remote(
            o_four.at[rel], att.at[:, columns(x)], s_of.at[rel - 1], r_of.at[rel - 1], at_slot(slot)
        )

    def out_eight(rel):
        slot = slot_of(rel)
        return remote(
            o_eight.at[rel], att.at[:, columns(X + here)], s_oe.at[rel - 1], r_oe.at[0],
            at_slot(slot),
        )

    def write_out(part):
        span = pl.ds(X * HEAD * part, X * HEAD * (part + 1))
        return pltpu.make_async_copy(att.at[:, span], att_out.at[0, :, span], l_att.at[part])

    stage(0, 0).start()
    partners = [at_slot(slot_of(rel)) for rel in range(1, GROUP)] + [over_core]
    partners += [device(z, (x + dx) % X, (y + dy) % Y, core) for dx, dy in SQUARE if dy != 0]
    barrier = pltpu.get_barrier_semaphore()
    for to in partners:
        pl.semaphore_signal(barrier, inc=1, device_id=to, device_id_type=MESH)
    for dz in range(1, Z):
        @pl.when((z + dz) % Z != 2 * frame + 1 - plane)
        def _(dz=dz):
            pl.semaphore_signal(barrier, inc=1, device_id=over_ring(dz), device_id_type=MESH)
    small = [
        pltpu.make_async_copy(src, dst, l_small.at[i])
        for i, (src, dst) in enumerate(
            (
                (up_in, up), (down_in, down_t), (order_in, order), (window_in, window),
                (valid_in, valid), (cot_in.at[0], cot),
            )
        )
    ]
    for part in range(3):
        for which in range(3):
            if (part, which) != (0, 0):
                stage(part, which).start()
    for move in small:
        move.start()
    pl.semaphore_wait(barrier, len(partners) + Z - 2)

    for which in range(2):
        stage(0, which).wait()
        fours[which][here] = staged[which][:, columns(x)]
        for rel in (2, 1, 3):
            four(which, rel).start()
            if rel == 2:
                over_z(which, 0).start()
    for which in range(3):
        for part in (1, 2):
            stage(part, which).wait()
        eight(which, 4).start()
    stage(0, 2).wait()
    q_four[x] = q_all[:, columns(x)]
    along = [four(2, rel) for rel in (2, 1, 3)]
    along += [eight(which, rel) for which in range(2) for rel in (2, 1, 3)]
    for rel in (1, 3, 2):
        for which in range(2):
            four(which, rel).wait_recv()
            over_z(which, rel).start()
            for c in along[:2 - which]:
                c.start()
            along = along[2 - which:]
    for other, rel in ((2, 6), (1, 5), (3, 7)):
        for which in range(2):
            eight(which, rel).start()
        eight(2, other).start()
    for rel in (6, 5, 7):
        eight(2, rel).start()
    for which in range(3):
        eights[which][here] = staged[which][:, columns(X + here)]
    for move in small:
        move.wait()
    back[...] = lax.dot_general(up[...], cot[...], NT, preferred_element_type=F32).astype(BF16)
    att[:, HEADS * HEAD:] = jnp.zeros((TILE, HEAD), BF16)

    half = TILE // 2
    lane = lax.broadcasted_iota(jnp.int32, (1, TILE), 1)
    row = lax.broadcasted_iota(jnp.int32, (half, HEAD), 0)

    def window_of(slot, key_of, value_of):
        tile = order[0, GROUP * frame + slot]
        keys, values, biases = [], [], []
        for entry in range(WIN):
            wanted = window[entry, 0, tile]
            present = wanted >= 0
            known = jnp.maximum(wanted, 0)
            first = known // 2 * 2
            there = jnp.where(order[0, first] == known, first, first + 1) - frame * GROUP
            there = jnp.where(present, jnp.clip(there, 0, GROUP - 1), here)
            count = jnp.where(present, valid[0, known], 0)
            keys.append(key_of[there])
            values.append(value_of[there])
            biases.append(jnp.where(lane < count, 0.0, -1e30).astype(F32))
        return keys, values, biases, valid[0, tile]

    def scores_of(query, keys, biases):
        scores = lax.dot_general(
            query, jnp.concatenate(keys, axis=0), NT, preferred_element_type=F32
        )
        return [scores[:, TILE * i:TILE * (i + 1)] + bias for i, bias in enumerate(biases)]

    def attend(scores, values, mine, start):
        top = jnp.max(functools.reduce(jnp.maximum, scores), axis=1, keepdims=True)
        weights = [jnp.exp2((each - top) * SCALE).astype(BF16) for each in scores]
        value = jnp.concatenate(values, axis=0)
        value = jnp.concatenate([value, jnp.ones_like(value)], axis=1)
        total = jnp.dot(jnp.concatenate(weights, axis=1), value, preferred_element_type=F32)
        return jnp.where(start + row < mine, total[:, :HEAD] / total[:, HEAD:], 0.0).astype(BF16)

    def units(tiles, key_of, value_of):
        jobs = []
        for slot, query_of, out, send in tiles:
            keys, values, biases, mine = window_of(slot, key_of, value_of)
            for start in (0, half):
                jobs.append((query_of, keys, values, biases, mine, start, out, send))
        ready = scores_of(jobs[0][0][pl.ds(0, half), :], jobs[0][1], jobs[0][3])
        for i, (_, _, values, _, mine, start, out, send) in enumerate(jobs):
            scores = ready
            if i + 1 < len(jobs):
                query_of, keys, _, biases, _, later = jobs[i + 1][:6]
                ready = scores_of(query_of[pl.ds(later, half), :], keys, biases)
            out[pl.ds(start, half), :] = attend(scores, values, mine, start)
        for tile in tiles:
            tile[3]()

    def collect(first, last):
        span = slice(first * HEAD, last * HEAD)
        term = lax.dot_general(down_t[:, span], att[:, span], NT, preferred_element_type=F32)
        hidden[...] = term if first == 0 else hidden[...] + term

    for rel in range(1, X):
        four(2, rel).wait_recv()
    for rel in range(X):
        for which in range(2):
            over_z(which, rel).wait_recv()

    def four_tile(rel):
        slot = slot_of(rel)
        send = out_four(rel).start if rel > 0 else lambda: None
        return slot, q_four.at[slot % X], o_four.at[rel], send

    units([four_tile(rel) for rel in (2, 1, 3, 0)], k_four, v_four)
    att[:, columns(x)] = o_four[0]

    for which in range(2):
        for rel in range(1, GROUP):
            eight(which, rel).wait_recv()

    def eight_tile(rel):
        slot = slot_of(rel)

        def send():
            @pl.when(rel != 0)
            def _():
                out_eight(rel).start()

        return slot, q_eight.at[slot], o_eight.at[rel], send

    def eight_pair(step, _):
        pair = (2 * step + 1, (2 * step + 2) % GROUP)
        for rel in pair:
            @pl.when(rel != 0)
            def _(rel=rel):
                eight(2, rel).wait_recv()

        units([eight_tile(rel) for rel in pair], k_eight, v_eight)

        @pl.when(step == 1)
        def _():
            for other in range(1, X):
                out_four(other).wait_recv()
            write_out(0).start()
            collect(0, X)

        return 0

    lax.fori_loop(0, GROUP // 2, eight_pair, 0)
    att[:, columns(X + here)] = o_eight[0]
    results = o_eight.at[pl.ds(1, GROUP - 1)]
    remote(results, results, s_oe.at[0], r_oe.at[0], over_core).wait_recv()
    write_out(1).start()
    collect(X, HEADS)

    mix = hidden[...].astype(BF16)

    band = acc.shape[1] // Y

    def rows_of(there):
        return pl.ds(pl.multiple_of(there * band, band), band)

    def over_square(dx, dy):
        return device(z, (x + dx) % X, (y + dy) % Y, core)

    def fill(ref, dx, owner):
        i = (x + dx) % X
        from_b = pl.ds(pl.multiple_of((2 * i + owner) * PART_B, HEAD), PART_B)
        from_a = pl.ds(pl.multiple_of(3 * HEAD * i + PART_A * owner, HEAD), PART_A)
        ref[dx, :, :PART_B] = jnp.dot(mix, cot[:, from_b], preferred_element_type=F32).astype(ref.dtype)
        ref[dx, :, PART_B:] = jnp.dot(
            back[...], att[:, from_a], preferred_element_type=F32
        ).astype(ref.dtype)

    def swap(dx):
        return remote(give.at[dx], got.at[dx], s_0.at[dx], r_0.at[dx], over_core)

    scatter = [
        remote(
            acc.at[dx, rows_of((y + dy) % Y)], parts.at[i], s_1.at[0], r_1.at[0],
            over_square(dx, dy),
        )
        for i, (dx, dy) in enumerate(SQUARE)
    ]
    for dx in FAR_FIRST:
        fill(give, dx, 1 - core)
        swap(dx).start()
    for dx in FAR_FIRST:
        fill(keep, dx, core)
        swap(dx).wait_recv()
        acc[dx] = (keep[dx] + got[dx].astype(F32)).astype(BF16)
        for c, (to, _) in zip(scatter, SQUARE):
            if to == dx:
                c.start()
    for part in range(2):
        write_out(part).wait()
    for which in range(3):
        for rel in range(1, X):
            four(which, rel).wait_send()
        for rel in range(1, GROUP):
            eight(which, rel).wait_send()
    for which in range(2):
        for rel in range(X):
            over_z(which, rel).wait_send()
    for rel in range(1, X):
        out_four(rel).wait_send()
    for rel in range(1, GROUP):
        out_eight(rel).wait_send()
    for dx in range(X):
        swap(dx).wait_send()
    all_parts = remote(parts, parts, s_1.at[0], r_1.at[0], over_core)
    all_parts.wait_recv()
    piece = acc[0, rows_of(y)].astype(F32)
    for i in range(len(SQUARE)):
        piece += parts[i].astype(F32)
    sums[z] = piece.astype(BF16)

    ring = [
        remote(sums.at[z], sums.at[z], s_2.at[0], r_2.at[0], over_ring(dz))
        for dz in (4, 3, 5, 2, 6, 1, 7)
    ]
    for c in ring:
        c.start()
    all_parts.wait_send()
    seven = sums.at[pl.ds(0, Z - 1)]
    all_ring = remote(seven, seven, s_2.at[0], r_2.at[0], over_core)
    all_ring.wait()
    total = sums[0].astype(F32)
    for i in range(1, Z):
        total += sums[i].astype(F32)
    final[core, x, rows_of(y), :] = total.astype(BF16)

    gather = [
        remote(
            final.at[core, x, rows_of(y)], final.at[core, x, rows_of(y)],
            s_3.at[dx], r_3.at[dx], over_square(dx, dy),
        )
        for i, (dx, dy) in enumerate(SQUARE)
    ]
    def pass_core(dx):
        ref = final.at[core, (x - dx + X) % X]
        return remote(ref, ref, s_4.at[dx], r_4.at[dx], over_core)

    def save(owner, dx):
        i = (x - dx + X) % X
        return pltpu.make_async_copy(final.at[owner, i], sum_out.at[owner, i], l_sum.at[owner, dx])

    gathered = []
    for dx in range(X):
        some = parts.at[pl.ds(0, Y if dx > 0 else Y - 1)]
        gathered.append(remote(some, some, s_3.at[dx], r_3.at[dx], over_core))
    for c in gather:
        c.start()
    for dx in (0, 1, 3, 2):
        gathered[dx].wait_recv()
        pass_core(dx).start()
        save(core, dx).start()
    for dx in (0, 1, 3, 2):
        pass_core(dx).wait_recv()
        save(1 - core, dx).start()
    for dx in range(X):
        gathered[dx].wait_send()
        pass_core(dx).wait_send()
        save(core, dx).wait()
        save(1 - core, dx).wait()


def attend_and_sum(order, window, valid, queries, keys, values, cotangent, down, up):
    hbm = pl.BlockSpec(memory_space=pl.ANY)
    dma = pltpu.SemaphoreType.DMA
    rank, wide = up.shape
    width = HEADS * HEAD
    near = len(SQUARE)

    def tiles(count):
        return pltpu.VMEM((count, TILE, HEAD), BF16)

    return pl.pallas_call(
        kernel,
        out_shape=(
            jax.ShapeDtypeStruct(queries.shape, BF16),
            jax.ShapeDtypeStruct((2, X, rank, PART), BF16),
        ),
        in_specs=[hbm] * 9,
        out_specs=(hbm, hbm),
        scratch_shapes=[pltpu.SMEM(t.shape, t.dtype) for t in (order, window, valid)]
        + [pltpu.VMEM(down.shape, BF16), pltpu.VMEM(up.shape, BF16)]
        + [tiles(GROUP), tiles(GROUP), tiles(X), tiles(X)]
        + [tiles(GROUP)] * 4
        + [pltpu.VMEM((TILE, width), BF16)] * 3
        + [pltpu.VMEM((TILE, width + HEAD), BF16)]
        + [
            pltpu.VMEM((TILE, wide), BF16),
            pltpu.VMEM((rank, TILE), BF16),
            pltpu.VMEM((rank, TILE), F32),
        ]
        + [pltpu.VMEM((X, rank, PART), F32)]
        + [pltpu.VMEM((X, rank, PART), BF16)] * 3
        + [
            pltpu.VMEM((near, rank // Y, PART), BF16),
            pltpu.VMEM((Z, rank // Y, PART), BF16),
            pltpu.VMEM((2, X, rank, PART), BF16),
        ]
        + [dma((3, X - 1))] * 2
        + [dma((2, X))] * 2
        + [dma((3, GROUP - 1))] * 2
        + [dma((X - 1,))] * 2
        + [dma((GROUP - 1,))] * 2
        + [dma((3, 3)), dma((6,)), dma((2,)), dma((2, X))]
        + [dma((X,))] * 2
        + [dma((1,))] * 4
        + [dma((X,))] * 4,
        compiler_params=pltpu.CompilerParams(
            collective_id=0, has_side_effects=True, vmem_limit_bytes=VMEM_LIMIT
        ),
        name="attend",
    )(order, window, valid, queries, keys, values, cotangent, down, up)


def finish_kernel(
    att_in, sum_in, att_out, gb_out, ga_out, att, summed, gb, ga, l_att, o_att, l_sum, o_gb, o_ga
):
    rows = TILE // X
    take_sum, take_att, put_att, put_gb, put_ga = [], [], [], [], []
    for i in range(X):
        span = pl.ds(i * rows, rows)
        wide, head = pl.ds(2 * PART_B * i, 2 * PART_B), pl.ds(3 * HEAD * i, 3 * HEAD)
        take_sum.append(pltpu.make_async_copy(sum_in.at[:, i], summed.at[:, i], l_sum.at[i]))
        take_att.append(pltpu.make_async_copy(att_in.at[0, span], att.at[0, span], l_att.at[i]))
        put_att.append(pltpu.make_async_copy(att.at[0, span], att_out.at[0, span], o_att.at[i]))
        put_gb.append(pltpu.make_async_copy(gb.at[:, wide], gb_out.at[:, wide], o_gb.at[i]))
        put_ga.append(pltpu.make_async_copy(ga.at[:, head], ga_out.at[:, head], o_ga.at[i]))
    for i in range(X):
        take_sum[i].start()
        take_att[i].start()
    for i in range(X):
        take_sum[i].wait()
        for core in range(2):
            first = (2 * i + core) * PART_B
            gb[:, first:first + PART_B] = summed[core, i, :, :PART_B].astype(F32)
        for j in range(3):
            first, start = (3 * i + j) * HEAD, PART_B + j % 2 * HEAD
            ga[:, first:first + HEAD] = summed[j // 2, i, :, start:start + HEAD].astype(F32)
        put_gb[i].start()
        put_ga[i].start()
        take_att[i].wait()
        put_att[i].start()
    for i in range(X):
        put_gb[i].wait()
        put_ga[i].wait()
        put_att[i].wait()


def finish(attention, summed, wide):
    hbm = pl.BlockSpec(memory_space=pl.ANY)
    rank = summed.shape[2]
    shapes = ((attention.shape, BF16), ((rank, wide), F32), ((rank, HEADS * HEAD), F32))
    held = (shapes[0], (summed.shape, BF16), shapes[1], shapes[2])
    return pl.pallas_call(
        finish_kernel,
        out_shape=tuple(jax.ShapeDtypeStruct(*each) for each in shapes),
        in_specs=[hbm, hbm],
        out_specs=(hbm, hbm, hbm),
        scratch_shapes=[pltpu.VMEM(*each) for each in held] + [pltpu.SemaphoreType.DMA((X,))] * 5,
        compiler_params=pltpu.CompilerParams(vmem_limit_bytes=VMEM_LIMIT),
        name="finish",
    )(attention, summed)


def per_device(queries, keys, values, cotangent, down, up, order, window, valid):
    attention, summed = attend_and_sum(
        order, window.transpose(2, 0, 1), valid, queries, keys, values, cotangent, down.T, up
    )
    attention, grad_b, grad_a = finish(attention, summed, up.shape[1])
    return attention, grad_a.T, grad_b


def solution(mesh):
    placed = (
        P("dp", "seq", None),
        P("dp", "seq", None),
        P("dp", "seq", None),
        P("dp", "seq", None),
        P(),
        P(),
        P("dp", None),
        P("dp", None, None),
        P("dp", None),
    )
    return jax.shard_map(
        per_device,
        mesh=mesh,
        in_specs=placed,
        out_specs=(P("dp", "seq", None), P(), P()),
        check_vma=False,
    )
```

```python
import functools
import math

import jax
import jax.numpy as jnp
from jax import lax
from jax.experimental import pallas as pl
from jax.experimental.pallas import tpu as pltpu
from jax.sharding import PartitionSpec as P

HEAD = 128
HEADS = 12
TILE = 384
WIN = 6
X, Z, Y = 4, 8, 4
GROUP = 2 * X
SCALE = math.log2(math.e) / math.sqrt(HEAD)
NT = (((1,), (1,)), ((), ()))
MESH = pl.DeviceIdType.MESH
BF16, F32 = jnp.bfloat16, jnp.float32
VMEM_LIMIT = 58 * 2**20
PART_B = 384
PART_A = 256
PART = PART_B + PART_A
FAR_FIRST = (2, 1, 3, 0)
SQUARE = [(dx, dy) for dx in FAR_FIRST for dy in (2, 1, 3, 0) if (dx, dy) != (0, 0)]


def place():
    seq, dp = lax.axis_index("seq"), lax.axis_index("dp")
    return seq // X, seq % X, dp // 2, dp % 2


def device(z, x, y, core):
    return {"seq": z * X + x, "dp": y * 2 + core}


def columns(head):
    return pl.ds(pl.multiple_of(head * HEAD, HEAD), HEAD)


def remote(src, dst, send, recv, to):
    return pltpu.make_async_remote_copy(
        src_ref=src, dst_ref=dst, send_sem=send, recv_sem=recv, device_id=to, device_id_type=MESH
    )


def flip(a, b):
    return a + b - 2 * a * b


def kernel(
    order_in, window_in, valid_in, q_in, k_in, v_in, cot_in, down_in, up_in,
    att_out, sum_out,
    order, window, valid, down_t, up,
    k_four, v_four, q_four, o_four, k_eight, v_eight, q_eight, o_eight,
    k_all, v_all, q_all, att, cot, back, hidden,
    keep, give, got, acc, parts, sums, final,
    s_four, r_four, s_z, r_z, s_eight, r_eight, s_of, r_of, s_oe, r_oe,
    l_in, l_small, l_att, l_sum,
    s_0, r_0, s_1, r_1, s_2, r_2, s_3, r_3, s_4, r_4,
):
    z, x, y, core = place()
    frame, plane = z // 2, z % 2
    here = plane * X + x
    staged = (k_all, v_all, q_all)
    fours = (k_four, v_four, q_four)
    eights = (k_eight, v_eight, q_eight)

    def slot_of(rel):
        return (
            4 * flip(plane, rel // 4) + 2 * flip(x // 2, rel // 2 % 2) + flip(x % 2, rel % 2)
        )

    def at_slot(slot):
        return device(2 * frame + slot // X, slot % X, y, core)

    over_core = device(z, x, y, 1 - core)

    def over_ring(dz):
        return device((z + dz) % Z, x, y, core)

    def stage(part, which):
        width = X * HEAD
        span = pl.ds(part * width, width)
        return pltpu.make_async_copy(
            (k_in, v_in, q_in)[which].at[0, :, span], staged[which].at[:, span], l_in.at[part, which]
        )

    def four(which, rel):
        slot = slot_of(rel)
        dst = fours[which].at[here if which < 2 else x]
        return remote(
            staged[which].at[:, columns(slot % X)], dst,
            s_four.at[which, rel - 1], r_four.at[which, rel - 1], at_slot(slot),
        )

    def over_z(which, rel):
        ref = fours[which].at[slot_of(rel)]
        return remote(ref, ref, s_z.at[which, rel], r_z.at[which, rel], at_slot(slot_of(4)))

    def eight(which, rel):
        slot = slot_of(rel)
        return remote(
            staged[which].at[:, columns(X + slot)], eights[which].at[here],
            s_eight.at[which, rel - 1], r_eight.at[which, rel - 1], at_slot(slot),
        )

    def out_four(rel):
        slot = slot_of(rel)
        return remote(
            o_four.at[rel], att.at[:, columns(x)], s_of.at[rel - 1], r_of.at[rel - 1], at_slot(slot)
        )

    def out_eight(rel):
        slot = slot_of(rel)
        return remote(
            o_eight.at[rel], att.at[:, columns(X + here)], s_oe.at[rel - 1], r_oe.at[0],
            at_slot(slot),
        )

    def write_out(part):
        span = pl.ds(X * HEAD * part, X * HEAD * (part + 1))
        return pltpu.make_async_copy(att.at[:, span], att_out.at[0, :, span], l_att.at[part])

    stage(0, 0).start()
    partners = [at_slot(slot_of(rel)) for rel in range(1, GROUP)] + [over_core]
    partners += [device(z, (x + dx) % X, (y + dy) % Y, core) for dx, dy in SQUARE if dy != 0]
    barrier = pltpu.get_barrier_semaphore()
    for to in partners:
        pl.semaphore_signal(barrier, inc=1, device_id=to, device_id_type=MESH)
    for dz in range(1, Z):
        @pl.when((z + dz) % Z != 2 * frame + 1 - plane)
        def _(dz=dz):
            pl.semaphore_signal(barrier, inc=1, device_id=over_ring(dz), device_id_type=MESH)
    small = [
        pltpu.make_async_copy(src, dst, l_small.at[i])
        for i, (src, dst) in enumerate(
            (
                (up_in, up), (down_in, down_t), (order_in, order), (window_in, window),
                (valid_in, valid), (cot_in.at[0], cot),
            )
        )
    ]
    for part in range(3):
        for which in range(3):
            if (part, which) != (0, 0):
                stage(part, which).start()
    for move in small:
        move.start()
    pl.semaphore_wait(barrier, len(partners) + Z - 2)

    for which in range(2):
        stage(0, which).wait()
        fours[which][here] = staged[which][:, columns(x)]
        for rel in (2, 1, 3):
            four(which, rel).start()
            if rel == 2:
                over_z(which, 0).start()
    for which in range(3):
        for part in (1, 2):
            stage(part, which).wait()
        eight(which, 4).start()
    stage(0, 2).wait()
    q_four[x] = q_all[:, columns(x)]
    along = [four(2, rel) for rel in (2, 1, 3)]
    along += [eight(which, rel) for which in range(2) for rel in (2, 1, 3)]
    for rel in (1, 3, 2):
        for which in range(2):
            four(which, rel).wait_recv()
            over_z(which, rel).start()
            for c in along[:2 - which]:
                c.start()
            along = along[2 - which:]
    for other, rel in ((2, 6), (1, 5), (3, 7)):
        for which in range(2):
            eight(which, rel).start()
        eight(2, other).start()
    for rel in (6, 5, 7):
        eight(2, rel).start()
    for which in range(3):
        eights[which][here] = staged[which][:, columns(X + here)]
    for move in small:
        move.wait()
    back[...] = lax.dot_general(up[...], cot[...], NT, preferred_element_type=F32).astype(BF16)
    att[:, HEADS * HEAD:] = jnp.zeros((TILE, HEAD), BF16)

    half = TILE // 2
    lane = lax.broadcasted_iota(jnp.int32, (1, TILE), 1)
    row = lax.broadcasted_iota(jnp.int32, (half, HEAD), 0)

    def window_of(slot, key_of, value_of):
        tile = order[0, GROUP * frame + slot]
        keys, values, biases = [], [], []
        for entry in range(WIN):
            wanted = window[entry, 0, tile]
            present = wanted >= 0
            known = jnp.maximum(wanted, 0)
            first = known // 2 * 2
            there = jnp.where(order[0, first] == known, first, first + 1) - frame * GROUP
            there = jnp.where(present, jnp.clip(there, 0, GROUP - 1), here)
            count = jnp.where(present, valid[0, known], 0)
            keys.append(key_of[there])
            values.append(value_of[there])
            biases.append(jnp.where(lane < count, 0.0, -1e30).astype(F32))
        return keys, values, biases, valid[0, tile]

    def scores_of(query, keys, biases):
        scores = lax.dot_general(
            query, jnp.concatenate(keys, axis=0), NT, preferred_element_type=F32
        )
        return [scores[:, TILE * i:TILE * (i + 1)] + bias for i, bias in enumerate(biases)]

    def attend(scores, values, mine, start):
        top = jnp.max(functools.reduce(jnp.maximum, scores), axis=1, keepdims=True)
        weights = [jnp.exp2((each - top) * SCALE).astype(BF16) for each in scores]
        value = jnp.concatenate(values, axis=0)
        value = jnp.concatenate([value, jnp.ones_like(value)], axis=1)
        total = jnp.dot(jnp.concatenate(weights, axis=1), value, preferred_element_type=F32)
        return jnp.where(start + row < mine, total[:, :HEAD] / total[:, HEAD:], 0.0).astype(BF16)

    def units(tiles, key_of, value_of):
        jobs = []
        for slot, query_of, out, send in tiles:
            keys, values, biases, mine = window_of(slot, key_of, value_of)
            for start in (0, half):
                jobs.append((query_of, keys, values, biases, mine, start, out, send))
        ready = scores_of(jobs[0][0][pl.ds(0, half), :], jobs[0][1], jobs[0][3])
        for i, (_, _, values, _, mine, start, out, send) in enumerate(jobs):
            scores = ready
            if i + 1 < len(jobs):
                query_of, keys, _, biases, _, later = jobs[i + 1][:6]
                ready = scores_of(query_of[pl.ds(later, half), :], keys, biases)
            out[pl.ds(start, half), :] = attend(scores, values, mine, start)
        for tile in tiles:
            tile[3]()

    def collect(first, last):
        span = slice(first * HEAD, last * HEAD)
        term = lax.dot_general(down_t[:, span], att[:, span], NT, preferred_element_type=F32)
        hidden[...] = term if first == 0 else hidden[...] + term

    for rel in range(1, X):
        four(2, rel).wait_recv()
    for rel in range(X):
        for which in range(2):
            over_z(which, rel).wait_recv()

    def four_tile(rel):
        slot = slot_of(rel)
        send = out_four(rel).start if rel > 0 else lambda: None
        return slot, q_four.at[slot % X], o_four.at[rel], send

    units([four_tile(rel) for rel in (2, 1, 3, 0)], k_four, v_four)
    att[:, columns(x)] = o_four[0]

    for which in range(2):
        for rel in range(1, GROUP):
            eight(which, rel).wait_recv()

    def eight_tile(rel):
        slot = slot_of(rel)

        def send():
            @pl.when(rel != 0)
            def _():
                out_eight(rel).start()

        return slot, q_eight.at[slot], o_eight.at[rel], send

    def eight_pair(step, _):
        pair = (2 * step + 1, (2 * step + 2) % GROUP)
        for rel in pair:
            @pl.when(rel != 0)
            def _(rel=rel):
                eight(2, rel).wait_recv()

        units([eight_tile(rel) for rel in pair], k_eight, v_eight)

        @pl.when(step == 1)
        def _():
            for other in range(1, X):
                out_four(other).wait_recv()
            write_out(0).start()
            collect(0, X)

        return 0

    lax.fori_loop(0, GROUP // 2, eight_pair, 0)
    att[:, columns(X + here)] = o_eight[0]
    results = o_eight.at[pl.ds(1, GROUP - 1)]
    remote(results, results, s_oe.at[0], r_oe.at[0], over_core).wait_recv()
    write_out(1).start()
    collect(X, HEADS)

    mix = hidden[...].astype(BF16)

    band = acc.shape[1] // Y

    def rows_of(there):
        return pl.ds(pl.multiple_of(there * band, band), band)

    def over_square(dx, dy):
        return device(z, (x + dx) % X, (y + dy) % Y, core)

    def fill(ref, dx, owner):
        i = (x + dx) % X
        from_b = pl.ds(pl.multiple_of((2 * i + owner) * PART_B, HEAD), PART_B)
        from_a = pl.ds(pl.multiple_of(3 * HEAD * i + PART_A * owner, HEAD), PART_A)
        ref[dx, :, :PART_B] = jnp.dot(mix, cot[:, from_b], preferred_element_type=F32).astype(ref.dtype)
        ref[dx, :, PART_B:] = jnp.dot(
            back[...], att[:, from_a], preferred_element_type=F32
        ).astype(ref.dtype)

    def swap(dx):
        return remote(give.at[dx], got.at[dx], s_0.at[dx], r_0.at[dx], over_core)

    scatter = [
        remote(
            acc.at[dx, rows_of((y + dy) % Y)], parts.at[i], s_1.at[0], r_1.at[0],
            over_square(dx, dy),
        )
        for i, (dx, dy) in enumerate(SQUARE)
    ]
    for i in range(X + 1):
        if i < X:
            fill(give, FAR_FIRST[i], 1 - core)
            swap(FAR_FIRST[i]).start()
        if i > 0:
            dx = FAR_FIRST[i - 1]
            fill(keep, dx, core)
            swap(dx).wait_recv()
            acc[dx] = (keep[dx] + got[dx].astype(F32)).astype(BF16)
            for c, (to, _) in zip(scatter, SQUARE):
                if to == dx:
                    c.start()
    for part in range(2):
        write_out(part).wait()
    for which in range(3):
        for rel in range(1, X):
            four(which, rel).wait_send()
        for rel in range(1, GROUP):
            eight(which, rel).wait_send()
    for which in range(2):
        for rel in range(X):
            over_z(which, rel).wait_send()
    for rel in range(1, X):
        out_four(rel).wait_send()
    for rel in range(1, GROUP):
        out_eight(rel).wait_send()
    for dx in range(X):
        swap(dx).wait_send()
    all_parts = remote(parts, parts, s_1.at[0], r_1.at[0], over_core)
    all_parts.wait_recv()
    piece = acc[0, rows_of(y)].astype(F32)
    for i in range(len(SQUARE)):
        piece += parts[i].astype(F32)
    sums[z] = piece.astype(BF16)

    ring = [
        remote(sums.at[z], sums.at[z], s_2.at[0], r_2.at[0], over_ring(dz))
        for dz in (4, 3, 5, 2, 6, 1, 7)
    ]
    for c in ring:
        c.start()
    all_parts.wait_send()
    seven = sums.at[pl.ds(0, Z - 1)]
    all_ring = remote(seven, seven, s_2.at[0], r_2.at[0], over_core)
    all_ring.wait()
    total = sums[0].astype(F32)
    for i in range(1, Z):
        total += sums[i].astype(F32)
    final[core, x, rows_of(y), :] = total.astype(BF16)

    gather = [
        remote(
            final.at[core, x, rows_of(y)], final.at[core, x, rows_of(y)],
            s_3.at[dx], r_3.at[dx], over_square(dx, dy),
        )
        for i, (dx, dy) in enumerate(SQUARE)
    ]
    def pass_core(dx):
        ref = final.at[core, (x - dx + X) % X]
        return remote(ref, ref, s_4.at[dx], r_4.at[dx], over_core)

    def save(owner, dx):
        i = (x - dx + X) % X
        return pltpu.make_async_copy(final.at[owner, i], sum_out.at[owner, i], l_sum.at[owner, dx])

    gathered = []
    for dx in range(X):
        some = parts.at[pl.ds(0, Y if dx > 0 else Y - 1)]
        gathered.append(remote(some, some, s_3.at[dx], r_3.at[dx], over_core))
    for c in gather:
        c.start()
    for dx in (0, 1, 3, 2):
        gathered[dx].wait_recv()
        pass_core(dx).start()
        save(core, dx).start()
    for dx in (0, 1, 3, 2):
        pass_core(dx).wait_recv()
        save(1 - core, dx).start()
    for dx in range(X):
        gathered[dx].wait_send()
        pass_core(dx).wait_send()
        save(core, dx).wait()
        save(1 - core, dx).wait()


def attend_and_sum(order, window, valid, queries, keys, values, cotangent, down, up):
    hbm = pl.BlockSpec(memory_space=pl.ANY)
    dma = pltpu.SemaphoreType.DMA
    rank, wide = up.shape
    width = HEADS * HEAD
    near = len(SQUARE)

    def tiles(count):
        return pltpu.VMEM((count, TILE, HEAD), BF16)

    return pl.pallas_call(
        kernel,
        out_shape=(
            jax.ShapeDtypeStruct(queries.shape, BF16),
            jax.ShapeDtypeStruct((2, X, rank, PART), BF16),
        ),
        in_specs=[hbm] * 9,
        out_specs=(hbm, hbm),
        scratch_shapes=[pltpu.SMEM(t.shape, t.dtype) for t in (order, window, valid)]
        + [pltpu.VMEM(down.shape, BF16), pltpu.VMEM(up.shape, BF16)]
        + [tiles(GROUP), tiles(GROUP), tiles(X), tiles(X)]
        + [tiles(GROUP)] * 4
        + [pltpu.VMEM((TILE, width), BF16)] * 3
        + [pltpu.VMEM((TILE, width + HEAD), BF16)]
        + [
            pltpu.VMEM((TILE, wide), BF16),
            pltpu.VMEM((rank, TILE), BF16),
            pltpu.VMEM((rank, TILE), F32),
        ]
        + [pltpu.VMEM((X, rank, PART), F32)]
        + [pltpu.VMEM((X, rank, PART), BF16)] * 3
        + [
            pltpu.VMEM((near, rank // Y, PART), BF16),
            pltpu.VMEM((Z, rank // Y, PART), BF16),
            pltpu.VMEM((2, X, rank, PART), BF16),
        ]
        + [dma((3, X - 1))] * 2
        + [dma((2, X))] * 2
        + [dma((3, GROUP - 1))] * 2
        + [dma((X - 1,))] * 2
        + [dma((GROUP - 1,))] * 2
        + [dma((3, 3)), dma((6,)), dma((2,)), dma((2, X))]
        + [dma((X,))] * 2
        + [dma((1,))] * 4
        + [dma((X,))] * 4,
        compiler_params=pltpu.CompilerParams(
            collective_id=0, has_side_effects=True, vmem_limit_bytes=VMEM_LIMIT
        ),
        name="attend",
    )(order, window, valid, queries, keys, values, cotangent, down, up)


def finish_kernel(
    att_in, sum_in, att_out, gb_out, ga_out, att, summed, gb, ga, l_att, o_att, l_sum, o_gb, o_ga
):
    rows = TILE // X
    take_sum, take_att, put_att, put_gb, put_ga = [], [], [], [], []
    for i in range(X):
        span = pl.ds(i * rows, rows)
        wide, head = pl.ds(2 * PART_B * i, 2 * PART_B), pl.ds(3 * HEAD * i, 3 * HEAD)
        take_sum.append(pltpu.make_async_copy(sum_in.at[:, i], summed.at[:, i], l_sum.at[i]))
        take_att.append(pltpu.make_async_copy(att_in.at[0, span], att.at[0, span], l_att.at[i]))
        put_att.append(pltpu.make_async_copy(att.at[0, span], att_out.at[0, span], o_att.at[i]))
        put_gb.append(pltpu.make_async_copy(gb.at[:, wide], gb_out.at[:, wide], o_gb.at[i]))
        put_ga.append(pltpu.make_async_copy(ga.at[:, head], ga_out.at[:, head], o_ga.at[i]))
    for i in range(X):
        take_sum[i].start()
        take_att[i].start()
    for i in range(X):
        take_sum[i].wait()
        for core in range(2):
            first = (2 * i + core) * PART_B
            gb[:, first:first + PART_B] = summed[core, i, :, :PART_B].astype(F32)
        for j in range(3):
            first, start = (3 * i + j) * HEAD, PART_B + j % 2 * HEAD
            ga[:, first:first + HEAD] = summed[j // 2, i, :, start:start + HEAD].astype(F32)
        put_gb[i].start()
        put_ga[i].start()
        take_att[i].wait()
        put_att[i].start()
    for i in range(X):
        put_gb[i].wait()
        put_ga[i].wait()
        put_att[i].wait()


def finish(attention, summed, wide):
    hbm = pl.BlockSpec(memory_space=pl.ANY)
    rank = summed.shape[2]
    shapes = ((attention.shape, BF16), ((rank, wide), F32), ((rank, HEADS * HEAD), F32))
    held = (shapes[0], (summed.shape, BF16), shapes[1], shapes[2])
    return pl.pallas_call(
        finish_kernel,
        out_shape=tuple(jax.ShapeDtypeStruct(*each) for each in shapes),
        in_specs=[hbm, hbm],
        out_specs=(hbm, hbm, hbm),
        scratch_shapes=[pltpu.VMEM(*each) for each in held] + [pltpu.SemaphoreType.DMA((X,))] * 5,
        compiler_params=pltpu.CompilerParams(vmem_limit_bytes=VMEM_LIMIT),
        name="finish",
    )(attention, summed)


def per_device(queries, keys, values, cotangent, down, up, order, window, valid):
    attention, summed = attend_and_sum(
        order, window.transpose(2, 0, 1), valid, queries, keys, values, cotangent, down.T, up
    )
    attention, grad_b, grad_a = finish(attention, summed, up.shape[1])
    return attention, grad_a.T, grad_b


def solution(mesh):
    placed = (
        P("dp", "seq", None),
        P("dp", "seq", None),
        P("dp", "seq", None),
        P("dp", "seq", None),
        P(),
        P(),
        P("dp", None),
        P("dp", None, None),
        P("dp", None),
    )
    return jax.shard_map(
        per_device,
        mesh=mesh,
        in_specs=placed,
        out_specs=(P("dp", "seq", None), P(), P()),
        check_vma=False,
    )
```
